32 devices in a mesh: epoch: 8 (over y, x, core), tile: 4 (over z).
Axes of the slice: x: 2, y: 2, z: 4, core: 2. Of those that a mesh axis runs over, the one named last changes fastest.
Arguments:
- images: bfloat16 [1024, 8192], P('epoch', 'tile')
- coverage: int32 [1024, 64], P('epoch', 'tile'), may hold values from 0 to 128, as said below
Outputs:
- scale_ratio: float32 [1024, 1024], P('epoch', 'tile')
- sky_offset: float32 [1024, 1024], P('epoch', 'tile')
The draws below stay inside these ranges and needn't reach their ends.
Inputs may be any that keep to these rules, and one draw needn't show every extreme that they name: Covered pixels of a segment are its first ones; the mean coverage differs between groups of segments.
All inputs are finite; a program needn't handle non-finite values.
Results may differ from the reference program's by a relative error of at most 0.0003.
Values may be sent and summed in bfloat16 or wider, within the bound.
A program may use at most 64 MiB of HBM per device.

```python
import jax
import jax.numpy as jnp
from jax import lax

PIX_DEV = 2048
SEG = 128
EPOCHS = 1024
PIXELS = 8192
SEGMENTS = 64


def draw_images(key, part):
    keys = jax.random.split(jax.random.fold_in(key, 11), 4)
    gains = jnp.exp(jax.random.uniform(keys[0], (EPOCHS, 1), jnp.float32, -0.7, 0.7))
    sky_level = jax.random.uniform(keys[1], (EPOCHS, 1), jnp.float32, -1.0, 1.0)
    template = jax.random.normal(keys[2], (1, PIXELS), jnp.float32)
    noise = jax.random.normal(keys[3], (EPOCHS, PIXELS), jnp.float32)
    return (gains * template + sky_level + noise).astype(jnp.bfloat16)


def draw_coverage(key, part):
    keys = jax.random.split(jax.random.fold_in(key, 23), 3)
    groups = PIXELS // PIX_DEV
    per_group = PIX_DEV // SEG
    levels = jax.random.randint(keys[0], (groups,), 1, 5)
    levels = jnp.repeat(levels, per_group)
    raw = jax.random.randint(keys[1], (EPOCHS, SEGMENTS), 0, 65536)
    ceiling = levels * (SEG // 2) + 1
    counts = jnp.minimum(raw % ceiling[None, :], SEG)
    chosen = jax.random.randint(keys[2], (), 0, EPOCHS)
    rows_index = jnp.arange(EPOCHS, dtype=jnp.int32)[:, None]
    return jnp.where(rows_index == chosen, SEG, counts).astype(jnp.int32)


def setup_inputs(seed: int = 0) -> dict:
    streams_of = jax.random.split(jax.random.key(seed), 3)
    images = draw_images(jax.random.fold_in(streams_of[2], 71), 0)
    coverage = draw_coverage(jax.random.fold_in(streams_of[2], 71), 0)
    return {"images": images, "coverage": coverage}


def contract(left, right):
    return lax.dot_general(left, right, (((1,), (1,)), ((), ())), precision=lax.Precision.HIGHEST, preferred_element_type=jnp.float32)


def reference(images, coverage):
    total_epochs = images.shape[0]
    within = lax.broadcasted_iota(jnp.int32, (1, 1, SEG), 2)
    flags = (within < coverage[:, :, None]).reshape(total_epochs, -1).astype(jnp.float32)
    masked = images.astype(jnp.float32) * flags
    squared = lax.optimization_barrier((masked * masked).astype(jnp.bfloat16)).astype(jnp.float32)
    block_count = PIXELS // PIX_DEV

    def absorb(carried, index):
        first = index * PIX_DEV
        flag_cols = lax.dynamic_slice_in_dim(flags, first, PIX_DEV, 1)
        mask_cols = lax.dynamic_slice_in_dim(masked, first, PIX_DEV, 1)
        square_cols = lax.dynamic_slice_in_dim(squared, first, PIX_DEV, 1)
        terms = jnp.stack([contract(flag_cols, flag_cols), contract(mask_cols, flag_cols), contract(flag_cols, mask_cols), contract(mask_cols, mask_cols), contract(flag_cols, square_cols)])
        return carried + terms, None

    start_sums = jnp.zeros((5, total_epochs, total_epochs), jnp.float32)
    totals, _ = lax.scan(absorb, start_sums, jnp.arange(block_count, dtype=jnp.int32))
    intersection, flux_i, flux_j, cross, power_j = totals[0], totals[1], totals[2], totals[3], totals[4]
    spread = intersection * power_j - flux_j * flux_j
    covariance = intersection * cross - flux_i * flux_j
    scale_ratio = covariance / (spread + intersection + 1.0)
    sky_offset = (flux_i - scale_ratio * flux_j) / (intersection + 1.0)
    return scale_ratio, sky_offset
```

```python
import functools

import jax
import jax.numpy as jnp
from jax import lax
from jax.experimental import pallas as pl
from jax.experimental.pallas import tpu as pltpu
from jax.sharding import PartitionSpec as P

SEG = 128
MESH = pl.DeviceIdType.MESH


def kernel(
    n_epoch, n_tile, images, coverage, scale_out, sky_out,
    held, left, right, power, stage, own, up, down,
    cov_pad, cov_turn, cov_held, cov_rows, cov_cols, inter,
    img_send, img_recv, pass_send, relay_send, relay_recv, cov_send, cov_recv,
    row_send, row_recv, col_send, col_recv, up_send, up_recv, down_send, down_recv,
):
    rows, pixels = images.shape
    segs = pixels // SEG
    n_chip = n_epoch // 2
    blocks = own.shape[0]
    relay = n_chip == 4
    me = lax.axis_index("epoch")
    z = lax.axis_index("tile")
    chip, core = me // 2, me % 2
    sibling = chip * 2 + (1 - core)

    def partner(d):
        other, bit = 0, 1
        while bit < n_chip:
            other = other + ((chip // bit + d // bit) % 2) * bit
            bit *= 2
        return other

    def to_epoch(src, dst, send, recv, target):
        return pltpu.make_async_remote_copy(
            src_ref=src, dst_ref=dst, send_sem=send, recv_sem=recv,
            device_id={"epoch": target}, device_id_type=MESH,
        )

    def to_tile(src, dst, send, recv, target):
        return pltpu.make_async_remote_copy(
            src_ref=src, dst_ref=dst, send_sem=send, recv_sem=recv,
            device_id={"tile": target}, device_id_type=MESH,
        )

    barrier = pltpu.get_barrier_semaphore()
    for d in range(1, n_epoch):
        pl.semaphore_signal(
            barrier, inc=1, device_id={"epoch": (me + d) % n_epoch}, device_id_type=MESH
        )
    for d in range(1, n_tile):
        pl.semaphore_signal(
            barrier, inc=1, device_id={"tile": (z + d) % n_tile}, device_id_type=MESH
        )
    cov_pad[...] = jnp.zeros_like(cov_pad)
    cov_turn[...] = jnp.zeros_like(cov_turn)
    cov_pad[:, :segs] = coverage[...].astype(jnp.float32)
    cov_held[me] = cov_pad[...].T[:segs]
    cov_rows[z] = cov_held[me]
    pl.semaphore_wait(barrier, n_epoch + n_tile - 2)

    cov_copies = []
    for d in range(1, n_epoch):
        cov_copies.append(to_epoch(
            cov_held.at[me], cov_held.at[me], cov_send.at[d - 1], cov_recv.at[me],
            (me + d) % n_epoch,
        ))
    img_copies = []
    direct = [d for d in range(1, n_chip) if not (relay and d == 3)]
    img_copies.append(to_epoch(
        images, held.at[me], img_send.at[0], img_recv.at[me], sibling
    ))
    for d in direct:
        img_copies.append(to_epoch(
            images, held.at[me], img_send.at[d], img_recv.at[me], partner(d) * 2 + core
        ))
    row_copies = []
    for d in range(1, n_tile):
        row_copies.append(to_tile(
            cov_rows.at[z], cov_rows.at[z], row_send.at[d - 1], row_recv.at[z],
            (z + d) % n_tile,
        ))
    for copy in cov_copies + img_copies + row_copies:
        copy.start()

    def image_block(block):
        return to_epoch(
            held.at[block], held.at[block], pass_send.at[0], img_recv.at[block], sibling
        )

    def hand_over(d):
        block = partner(d) * 2 + core
        return to_epoch(
            held.at[block], held.at[block], pass_send.at[d], img_recv.at[block], sibling
        )

    half = rows // 2

    def relay_copy(d):
        block = partner(d) * 2 + core
        part = held.at[block, pl.ds((d - 1) * half, half)]
        return to_epoch(
            part, part, relay_send.at[d - 1], relay_recv.at[d - 1],
            partner(3 - d) * 2 + core,
        )

    def relay_arrived(d):
        block = partner(3) * 2 + core
        part = held.at[block, pl.ds((d - 1) * half, half)]
        return to_epoch(
            part, part, relay_send.at[d - 1], relay_recv.at[d - 1],
            partner(3 - d) * 2 + core,
        )

    lane = lax.broadcasted_iota(jnp.int32, (rows, SEG), 1).astype(jnp.float32)
    for s in range(segs):
        cols = slice(s * SEG, (s + 1) * SEG)
        flag = lane < cov_pad[:, s:s + 1]
        image = images[:, cols]
        held[me, :, cols] = image
        left[:rows, cols] = jnp.where(flag, image.astype(jnp.float32), 0.0).astype(jnp.bfloat16)
        left[rows:, cols] = jnp.where(flag, 1.0, 0.0).astype(jnp.bfloat16)

    def contract(a, b):
        return lax.dot_general(
            a, b, (((1,), (1,)), ((), ())), preferred_element_type=jnp.float32
        )

    parity = (chip % 2 + (chip // 2) % 2) % 2

    def step(n, carry):
        pair = n // 2
        d = jnp.where(
            (parity == 0) & (pair > 0), 1 + pair % (n_chip - 1), pair
        ) if relay else pair
        block = partner(d) * 2 + (core + n) % 2

        @pl.when(n == 2)
        def _():
            for e in direct:
                image_block(partner(e) * 2 + core).wait_recv()
                hand_over(e).start()
                if relay:
                    relay_copy(e).start()

        if relay:
            @pl.when((d == 3) & (n % 2 == 0))
            def _():
                relay_arrived(1).wait_recv()
                relay_arrived(2).wait_recv()
                hand_over(3).start()

        @pl.when(n % 2 == 1)
        def _():
            image_block(block).wait_recv()

        @pl.when(n == 1)
        def _():
            for e in range(1, n_epoch):
                other = (me + e) % n_epoch
                to_epoch(
                    cov_held.at[other], cov_held.at[other], cov_send.at[0],
                    cov_recv.at[other], other,
                ).wait_recv()
            for e in range(1, n_tile):
                target = (z + e) % n_tile
                for j in range(blocks):
                    to_tile(
                        cov_held.at[target * blocks + j], cov_cols.at[z, j],
                        col_send.at[e - 1, j], col_recv.at[z, j], target,
                    ).start()
            for j in range(blocks):
                cov_cols[z, j] = cov_held[z * blocks + j]

        cov_turn[:segs] = cov_held[block]
        cov_pad[...] = cov_turn[...].T
        for s in range(segs):
            cols = slice(s * SEG, (s + 1) * SEG)
            flag = lane < cov_pad[:, s:s + 1]
            masked = jnp.where(flag, held[block, :, cols].astype(jnp.float32), 0.0)
            right[:rows, cols] = masked.astype(jnp.bfloat16)
            right[rows:, cols] = jnp.where(flag, 1.0, 0.0).astype(jnp.bfloat16)
            power[:, cols] = (masked * masked).astype(jnp.bfloat16)

        sums = contract(left[...], right[...])
        stage[0] = sums[:rows, :rows]
        stage[1] = sums[:rows, rows:]
        stage[2] = sums[rows:, :rows]
        stage[3] = contract(left[rows:, :], power[...])

        target = block // blocks

        @pl.when(z == target)
        def _():
            own[block % blocks] = stage[...]

        @pl.when(z < target)
        def _():
            copy = to_tile(
                up.at[block], up.at[block], up_send.at[block], up_recv.at[block],
                jnp.minimum(z + 1, n_tile - 1),
            )

            @pl.when(z == 0)
            def _():
                up[block] = stage[...]

            @pl.when(z > 0)
            def _():
                copy.wait_recv()
                up[block] = up[block] + stage[...]

            copy.start()

        @pl.when(z > target)
        def _():
            copy = to_tile(
                down.at[block], down.at[block], down_send.at[block], down_recv.at[block],
                jnp.maximum(z - 1, 0),
            )

            @pl.when(z == n_tile - 1)
            def _():
                down[block] = stage[...]

            @pl.when(z < n_tile - 1)
            def _():
                copy.wait_recv()
                down[block] = down[block] + stage[...]

            copy.start()

        return carry

    lax.fori_loop(0, n_epoch, step, 0)

    for e in range(1, n_tile):
        other = (z + e) % n_tile
        to_tile(
            cov_rows.at[other], cov_rows.at[other], row_send.at[0], row_recv.at[other], other
        ).wait_recv()
        for j in range(blocks):
            to_tile(
                cov_cols.at[other, j], cov_cols.at[other, j], col_send.at[0, j],
                col_recv.at[other, j], other,
            ).wait_recv()
    inter[...] = jnp.zeros_like(inter)

    def overlap(t, carry):
        cov_turn[:segs] = cov_rows[t]
        cov_pad[...] = cov_turn[...].T
        for j in range(blocks):
            cols = slice(j * rows, (j + 1) * rows)
            total = inter[:, cols]
            for s in range(segs):
                total = total + jnp.minimum(cov_pad[:, s:s + 1], cov_cols[t, j, s:s + 1, :])
            inter[:, cols] = total
        return carry

    lax.fori_loop(0, n_tile, overlap, 0)

    for j in range(blocks):
        block = z * blocks + j

        @pl.when(z > 0)
        def _():
            to_tile(
                up.at[block], up.at[block], up_send.at[block], up_recv.at[block],
                jnp.maximum(z - 1, 0),
            ).wait_recv()
            own[j] = own[j] + up[block]

        @pl.when(z < n_tile - 1)
        def _():
            to_tile(
                down.at[block], down.at[block], down_send.at[block], down_recv.at[block],
                jnp.minimum(z + 1, n_tile - 1),
            ).wait_recv()
            own[j] = own[j] + down[block]

        cols = slice(j * rows, (j + 1) * rows)
        intersection = inter[:, cols]
        cross, flux_i, flux_j, power_j = own[j, 0], own[j, 1], own[j, 2], own[j, 3]
        spread = intersection * power_j - flux_j * flux_j
        covariance = intersection * cross - flux_i * flux_j
        scale_ratio = covariance / (spread + intersection + 1.0)
        scale_out[:, cols] = scale_ratio
        sky_out[:, cols] = (flux_i - scale_ratio * flux_j) / (intersection + 1.0)

    for copy in cov_copies + img_copies + row_copies:
        copy.wait_send()
    for d in range(1, n_chip):
        hand_over(d).wait_send()
    if relay:
        relay_copy(1).wait_send()
        relay_copy(2).wait_send()
    for e in range(1, n_tile):
        target = (z + e) % n_tile
        for j in range(blocks):
            to_tile(
                cov_held.at[target * blocks + j], cov_cols.at[z, j],
                col_send.at[e - 1, j], col_recv.at[z, j], target,
            ).wait_send()

    def drain(block, carry):
        target = block // blocks

        @pl.when(z < target)
        def _():
            to_tile(
                up.at[block], up.at[block], up_send.at[block], up_recv.at[block],
                jnp.minimum(z + 1, n_tile - 1),
            ).wait_send()

        @pl.when(z > target)
        def _():
            to_tile(
                down.at[block], down.at[block], down_send.at[block], down_recv.at[block],
                jnp.maximum(z - 1, 0),
            ).wait_send()

        return carry

    lax.fori_loop(0, n_epoch, drain, 0)


def solution(mesh):
    n_epoch, n_tile = mesh.shape["epoch"], mesh.shape["tile"]

    def body(images, coverage):
        rows, pixels = images.shape
        segs = coverage.shape[1]
        width = rows * n_epoch // n_tile
        blocks = width // rows
        dma, f32 = pltpu.SemaphoreType.DMA, jnp.float32
        out = jax.ShapeDtypeStruct((rows, width), f32)
        vmem = pl.BlockSpec(memory_space=pltpu.VMEM)
        return pl.pallas_call(
            functools.partial(kernel, n_epoch, n_tile),
            out_shape=(out, out),
            in_specs=[vmem, vmem],
            out_specs=(vmem, vmem),
            scratch_shapes=[
                pltpu.VMEM((n_epoch, rows, pixels), jnp.bfloat16),
                pltpu.VMEM((2 * rows, pixels), jnp.bfloat16),
                pltpu.VMEM((2 * rows, pixels), jnp.bfloat16),
                pltpu.VMEM((rows, pixels), jnp.bfloat16),
                pltpu.VMEM((4, rows, rows), f32),
                pltpu.VMEM((blocks, 4, rows, rows), f32),
                pltpu.VMEM((n_epoch, 4, rows, rows), f32),
                pltpu.VMEM((n_epoch, 4, rows, rows), f32),
                pltpu.VMEM((rows, SEG), f32),
                pltpu.VMEM((SEG, rows), f32),
                pltpu.VMEM((n_epoch, segs, rows), f32),
                pltpu.VMEM((n_tile, segs, rows), f32),
                pltpu.VMEM((n_tile, blocks, segs, rows), f32),
                pltpu.VMEM((rows, width), f32),
                dma((n_epoch // 2,)), dma((n_epoch,)), dma((n_epoch // 2,)),
                dma((2,)), dma((2,)), dma((n_epoch,)), dma((n_epoch,)),
                dma((n_tile,)), dma((n_tile,)),
                dma((n_tile, blocks)), dma((n_tile, blocks)),
                dma((n_epoch,)), dma((n_epoch,)), dma((n_epoch,)), dma((n_epoch,)),
            ],
            compiler_params=pltpu.CompilerParams(
                collective_id=0, has_side_effects=True, vmem_limit_bytes=48 * 1024 * 1024
            ),
        )(images, coverage)

    specs = (P("epoch", "tile"), P("epoch", "tile"))
    return jax.shard_map(body, mesh=mesh, in_specs=specs, out_specs=specs, check_vma=False)
```

```python
import functools

import jax
import jax.numpy as jnp
from jax import lax
from jax.experimental import pallas as pl
from jax.experimental.pallas import tpu as pltpu
from jax.sharding import PartitionSpec as P

SEG = 128
MESH = pl.DeviceIdType.MESH


def kernel(
    n_epoch, n_tile, images, coverage, scale_out, sky_out,
    held, left, right, power, parts, own, up, down,
    cov_pad, cov_turn, cov_held, cov_rows, cov_cols, inter,
    local_sem, img_send, img_recv, pass_send, relay_send, relay_recv, cov_send, cov_recv,
    row_send, row_recv, col_send, col_recv, up_send, up_recv, down_send, down_recv,
):
    rows, pixels = images.shape
    segs = pixels // SEG
    n_chip = n_epoch // 2
    blocks = own.shape[0]
    relay = n_chip == 4
    me = lax.axis_index("epoch")
    z = lax.axis_index("tile")
    chip, core = me // 2, me % 2
    sibling = chip * 2 + (1 - core)

    def partner(d):
        other, bit = 0, 1
        while bit < n_chip:
            other = other + ((chip // bit + d // bit) % 2) * bit
            bit *= 2
        return other

    def to_epoch(src, dst, send, recv, target):
        return pltpu.make_async_remote_copy(
            src_ref=src, dst_ref=dst, send_sem=send, recv_sem=recv,
            device_id={"epoch": target}, device_id_type=MESH,
        )

    def to_tile(src, dst, send, recv, target):
        return pltpu.make_async_remote_copy(
            src_ref=src, dst_ref=dst, send_sem=send, recv_sem=recv,
            device_id={"tile": target}, device_id_type=MESH,
        )

    fetch = pltpu.make_async_copy(images, held.at[me], local_sem)
    fetch.start()
    barrier = pltpu.get_barrier_semaphore()
    for d in range(1, n_epoch):
        pl.semaphore_signal(
            barrier, inc=1, device_id={"epoch": (me + d) % n_epoch}, device_id_type=MESH
        )
    for d in range(1, n_tile):
        pl.semaphore_signal(
            barrier, inc=1, device_id={"tile": (z + d) % n_tile}, device_id_type=MESH
        )
    cov_turn[...] = jnp.zeros_like(cov_turn)
    cov_held[me] = coverage[...].astype(jnp.float32)
    cov_rows[z] = cov_held[me]
    cov_turn[:segs] = cov_held[me]
    cov_pad[...] = cov_turn[...].T
    pl.semaphore_wait(barrier, n_epoch + n_tile - 2)

    cov_copies = []
    for d in range(1, n_epoch):
        cov_copies.append(to_epoch(
            cov_held.at[me], cov_held.at[me], cov_send.at[d - 1], cov_recv.at[me],
            (me + d) % n_epoch,
        ))
    def image_to(d):
        return to_epoch(
            images, held.at[me], img_send.at[d], img_recv.at[me], partner(d) * 2 + core
        )

    to_sibling = to_epoch(images, held.at[me], img_send.at[0], img_recv.at[me], sibling)
    first, second = 1 + core, 2 - core
    start_now = [image_to(first)] if relay else [image_to(d) for d in range(1, n_chip)]
    row_copies = []
    for d in range(1, n_tile):
        row_copies.append(to_tile(
            cov_rows.at[z], cov_rows.at[z], row_send.at[d - 1], row_recv.at[z],
            (z + d) % n_tile,
        ))
    for copy in start_now + [to_sibling] + cov_copies + row_copies:
        copy.start()

    def image_block(block):
        return to_epoch(
            held.at[block], held.at[block], pass_send.at[0], img_recv.at[block], sibling
        )

    def hand_over(d):
        block = partner(d) * 2 + core
        return to_epoch(
            held.at[block], held.at[block], pass_send.at[d], img_recv.at[block], sibling
        )

    half = rows // 2

    def relay_copy(d):
        block = partner(d) * 2 + core
        part = held.at[block, pl.ds(pl.multiple_of((d - 1) * half, half), half)]
        return to_epoch(
            part, part, relay_send.at[d - 1], relay_recv.at[d - 1],
            partner(3 - d) * 2 + core,
        )

    def relay_arrived(d):
        block = partner(3) * 2 + core
        part = held.at[block, pl.ds((d - 1) * half, half)]
        return to_epoch(
            part, part, relay_send.at[d - 1], relay_recv.at[d - 1],
            partner(3 - d) * 2 + core,
        )

    def pass_on(d):
        image_block(partner(d) * 2 + core).wait_recv()
        hand_over(d).start()
        if relay:
            relay_copy(d).start()

    def up_copy(block, i, target):
        ref = up.at[block, i]
        return to_tile(ref, ref, up_send.at[block, i], up_recv.at[block, i], target)

    def down_copy(block, i, target):
        ref = down.at[block, i]
        return to_tile(ref, ref, down_send.at[block, i], down_recv.at[block, i], target)

    above, below = jnp.minimum(z + 1, n_tile - 1), jnp.maximum(z - 1, 0)

    fetch.wait()
    lane = lax.broadcasted_iota(jnp.int32, (rows, SEG), 1).astype(jnp.float32)
    for s in range(segs):
        cols = slice(s * SEG, (s + 1) * SEG)
        flag = lane < cov_pad[:, s:s + 1]
        image = held[me, :, cols]
        left[:rows, cols] = jnp.where(flag, image.astype(jnp.float32), 0.0).astype(jnp.bfloat16)
        left[rows:, cols] = jnp.where(flag, 1.0, 0.0).astype(jnp.bfloat16)

    def contract(a, b):
        return lax.dot_general(
            a, b, (((1,), (1,)), ((), ())), preferred_element_type=jnp.float32
        )

    outer = (chip % 2 + chip // 2) % 2 == 0 if relay else None

    def place(n):
        if not relay:
            return n // 2, (core + n) % 2
        near, late = n % 2, n // 4
        diagonal = jnp.where(outer, n // 2 == 2, n // 2 == 3)
        d = jnp.where(
            late == 0,
            jnp.where(n < 2, 0, jnp.where(near == 0, first, second)),
            jnp.where(diagonal, 3, 2 - near),
        )
        k = jnp.where((late == 0) | diagonal, (core + n) % 2, near)
        return d, k

    def compute(n):
        d, k = place(n)
        block = partner(d) * 2 + k

        @pl.when(n == 2)
        def _():
            if relay:
                pass_on(first)
                image_to(first).wait_send()
                image_to(second).start()
            else:
                for e in range(1, n_chip):
                    pass_on(e)

        if relay:
            @pl.when(n == 4)
            def _():
                pass_on(second)

            @pl.when((d == 3) & (k == core))
            def _():
                relay_arrived(1).wait_recv()
                relay_arrived(2).wait_recv()
                hand_over(3).start()

        @pl.when(k != core)
        def _():
            image_block(block).wait_recv()

        @pl.when(n == 1)
        def _():
            for e in range(1, n_epoch):
                other = (me + e) % n_epoch
                to_epoch(
                    cov_held.at[other], cov_held.at[other], cov_send.at[0],
                    cov_recv.at[other], other,
                ).wait_recv()
            for e in range(1, n_tile):
                target = (z + e) % n_tile
                for j in range(blocks):
                    to_tile(
                        cov_held.at[target * blocks + j], cov_cols.at[z, j],
                        col_send.at[e - 1, j], col_recv.at[z, j], target,
                    ).start()
            for j in range(blocks):
                cov_cols[z, j] = cov_held[z * blocks + j]

        cov_turn[:segs] = cov_held[block]
        cov_pad[...] = cov_turn[...].T
        for s in range(segs):
            cols = slice(s * SEG, (s + 1) * SEG)
            flag = lane < cov_pad[:, s:s + 1]
            masked = jnp.where(flag, held[block, :, cols].astype(jnp.float32), 0.0)
            right[:rows, cols] = masked.astype(jnp.bfloat16)
            right[rows:, cols] = jnp.where(flag, 1.0, 0.0).astype(jnp.bfloat16)
            power[:, cols] = (masked * masked).astype(jnp.bfloat16)

        sums = contract(left[...], right[...])
        parts[block, 0] = sums[:rows, :rows]
        parts[block, 1] = sums[:rows, rows:]
        parts[block, 2] = sums[rows:, :rows]
        parts[block, 3] = contract(left[rows:, :], power[...])

        target = block // blocks

        @pl.when(z == target)
        def _():
            own[block % blocks] = parts[block]

        @pl.when((z == 0) & (target > 0))
        def _():
            up[block] = parts[block]
            for i in range(4):
                up_copy(block, i, above).start()

        @pl.when((z == n_tile - 1) & (target < n_tile - 1))
        def _():
            down[block] = parts[block]
            for i in range(4):
                down_copy(block, i, below).start()

    def forward(n):
        d, k = place(n)
        block = partner(d) * 2 + k
        target = block // blocks

        @pl.when((z > 0) & (z < target))
        def _():
            for i in range(4):
                up_copy(block, i, above).wait_recv()
                up[block, i] = up[block, i] + parts[block, i]
                up_copy(block, i, above).start()

        @pl.when((z < n_tile - 1) & (z > target))
        def _():
            for i in range(4):
                down_copy(block, i, below).wait_recv()
                down[block, i] = down[block, i] + parts[block, i]
                down_copy(block, i, below).start()

    def intersect():
        for e in range(1, n_tile):
            other = (z + e) % n_tile
            to_tile(
                cov_rows.at[other], cov_rows.at[other], row_send.at[0], row_recv.at[other], other
            ).wait_recv()
            for j in range(blocks):
                to_tile(
                    cov_cols.at[other, j], cov_cols.at[other, j], col_send.at[0, j],
                    col_recv.at[other, j], other,
                ).wait_recv()
        inter[...] = jnp.zeros_like(inter)

        def overlap(t, carry):
            cov_turn[:segs] = cov_rows[t]
            cov_pad[...] = cov_turn[...].T
            for j in range(blocks):
                cols = slice(j * rows, (j + 1) * rows)
                total = inter[:, cols]
                for s in range(segs):
                    total = total + jnp.minimum(cov_pad[:, s:s + 1], cov_cols[t, j, s:s + 1, :])
                inter[:, cols] = total
            return carry

        lax.fori_loop(0, n_tile, overlap, 0)

    lag = 2

    def step(n, carry):
        @pl.when(n < n_epoch)
        def _():
            compute(n)

        @pl.when(n == n_epoch - 3)
        def _():
            intersect()

        @pl.when(n >= lag)
        def _():
            forward(n - lag)

        return carry

    lax.fori_loop(0, n_epoch + lag, step, 0)

    for j in range(blocks):
        block = z * blocks + j

        @pl.when(z > 0)
        def _():
            for i in range(4):
                up_copy(block, i, below).wait_recv()
            own[j] = own[j] + up[block]

        @pl.when(z < n_tile - 1)
        def _():
            for i in range(4):
                down_copy(block, i, above).wait_recv()
            own[j] = own[j] + down[block]

        cols = slice(j * rows, (j + 1) * rows)
        intersection = inter[:, cols]
        cross, flux_i, flux_j, power_j = own[j, 0], own[j, 1], own[j, 2], own[j, 3]
        spread = intersection * power_j - flux_j * flux_j
        covariance = intersection * cross - flux_i * flux_j
        scale_ratio = covariance / (spread + intersection + 1.0)
        scale_out[:, cols] = scale_ratio
        sky_out[:, cols] = (flux_i - scale_ratio * flux_j) / (intersection + 1.0)

    late = [image_to(second)] if relay else start_now
    for copy in late + [to_sibling] + cov_copies + row_copies:
        copy.wait_send()
    for d in range(1, n_chip):
        hand_over(d).wait_send()
    if relay:
        relay_copy(1).wait_send()
        relay_copy(2).wait_send()
    for e in range(1, n_tile):
        target = (z + e) % n_tile
        for j in range(blocks):
            to_tile(
                cov_held.at[target * blocks + j], cov_cols.at[z, j],
                col_send.at[e - 1, j], col_recv.at[z, j], target,
            ).wait_send()

    def drain(block, carry):
        target = block // blocks

        @pl.when(z < target)
        def _():
            for i in range(4):
                up_copy(block, i, above).wait_send()

        @pl.when(z > target)
        def _():
            for i in range(4):
                down_copy(block, i, below).wait_send()

        return carry

    lax.fori_loop(0, n_epoch, drain, 0)


def solution(mesh):
    n_epoch, n_tile = mesh.shape["epoch"], mesh.shape["tile"]

    def body(images, coverage):
        rows, pixels = images.shape
        segs = coverage.shape[1]
        width = rows * n_epoch // n_tile
        blocks = width // rows
        dma, f32 = pltpu.SemaphoreType.DMA, jnp.float32
        out = jax.ShapeDtypeStruct((rows, width), f32)
        vmem = pl.BlockSpec(memory_space=pltpu.VMEM)
        return pl.pallas_call(
            functools.partial(kernel, n_epoch, n_tile),
            out_shape=(out, out),
            in_specs=[pl.BlockSpec(memory_space=pltpu.HBM), vmem],
            out_specs=(vmem, vmem),
            scratch_shapes=[
                pltpu.VMEM((n_epoch, rows, pixels), jnp.bfloat16),
                pltpu.VMEM((2 * rows, pixels), jnp.bfloat16),
                pltpu.VMEM((2 * rows, pixels), jnp.bfloat16),
                pltpu.VMEM((rows, pixels), jnp.bfloat16),
                pltpu.VMEM((n_epoch, 4, rows, rows), f32),
                pltpu.VMEM((blocks, 4, rows, rows), f32),
                pltpu.VMEM((n_epoch, 4, rows, rows), f32),
                pltpu.VMEM((n_epoch, 4, rows, rows), f32),
                pltpu.VMEM((rows, SEG), f32),
                pltpu.VMEM((SEG, rows), f32),
                pltpu.VMEM((n_epoch, segs, rows), f32),
                pltpu.VMEM((n_tile, segs, rows), f32),
                pltpu.VMEM((n_tile, blocks, segs, rows), f32),
                pltpu.VMEM((rows, width), f32),
                dma, dma((n_epoch // 2,)), dma((n_epoch,)), dma((n_epoch // 2,)),
                dma((2,)), dma((2,)), dma((n_epoch,)), dma((n_epoch,)),
                dma((n_tile,)), dma((n_tile,)),
                dma((n_tile, blocks)), dma((n_tile, blocks)),
                dma((n_epoch, 4)), dma((n_epoch, 4)), dma((n_epoch, 4)), dma((n_epoch, 4)),
            ],
            compiler_params=pltpu.CompilerParams(
                collective_id=0, has_side_effects=True, vmem_limit_bytes=48 * 1024 * 1024
            ),
        )(images, coverage.T)

    specs = (P("epoch", "tile"), P("epoch", "tile"))
    return jax.shard_map(body, mesh=mesh, in_specs=specs, out_specs=specs, check_vma=False)
```

```python
import functools

import jax
import jax.numpy as jnp
from jax import lax
from jax.experimental import pallas as pl
from jax.experimental.pallas import tpu as pltpu
from jax.sharding import PartitionSpec as P

SEG = 128
MESH = pl.DeviceIdType.MESH


def kernel(
    n_epoch, n_tile, images, coverage, scale_out, sky_out,
    held, left, right, parts, own, up, down,
    cov_own, cov_pad, cov_turn, cov_held, cov_rows, cov_cols, inter,
    local_sem, img_send, img_recv, pass_send, relay_send, relay_recv, cov_send, cov_recv,
    row_send, row_recv, col_send, col_recv, up_send, up_recv, down_send, down_recv,
):
    rows, pixels = images.shape
    segs = pixels // SEG
    n_chip = n_epoch // 2
    blocks = own.shape[0]
    relay = n_chip == 4
    me = lax.axis_index("epoch")
    z = lax.axis_index("tile")
    chip, core = me // 2, me % 2
    sibling = chip * 2 + (1 - core)

    def partner(d):
        other, bit = 0, 1
        while bit < n_chip:
            other = other + ((chip // bit + d // bit) % 2) * bit
            bit *= 2
        return other

    def to_epoch(src, dst, send, recv, target):
        return pltpu.make_async_remote_copy(
            src_ref=src, dst_ref=dst, send_sem=send, recv_sem=recv,
            device_id={"epoch": target}, device_id_type=MESH,
        )

    def to_tile(src, dst, send, recv, target):
        return pltpu.make_async_remote_copy(
            src_ref=src, dst_ref=dst, send_sem=send, recv_sem=recv,
            device_id={"tile": target}, device_id_type=MESH,
        )

    fetch_cov = pltpu.make_async_copy(coverage, cov_own, local_sem.at[1])
    fetch_cov.start()
    fetch = pltpu.make_async_copy(images, held.at[me], local_sem.at[0])
    fetch.start()
    barrier = pltpu.get_barrier_semaphore()
    for d in range(1, n_epoch):
        pl.semaphore_signal(
            barrier, inc=1, device_id={"epoch": (me + d) % n_epoch}, device_id_type=MESH
        )
    for d in range(1, n_tile):
        pl.semaphore_signal(
            barrier, inc=1, device_id={"tile": (z + d) % n_tile}, device_id_type=MESH
        )
    cov_turn[...] = jnp.zeros_like(cov_turn)
    fetch_cov.wait()
    cov_held[me] = cov_own[...].astype(jnp.float32)
    cov_rows[z] = cov_held[me]
    cov_turn[:segs] = cov_held[me]
    cov_pad[...] = cov_turn[...].T
    pl.semaphore_wait(barrier, n_epoch + n_tile - 2)

    cov_copies = []
    for d in range(1, n_epoch):
        cov_copies.append(to_epoch(
            cov_held.at[me], cov_held.at[me], cov_send.at[d - 1], cov_recv.at[me],
            (me + d) % n_epoch,
        ))
    def image_to(d):
        return to_epoch(
            images, held.at[me], img_send.at[d], img_recv.at[me], partner(d) * 2 + core
        )

    to_sibling = to_epoch(images, held.at[me], img_send.at[0], img_recv.at[me], sibling)
    first, second = 1 + core, 2 - core
    start_now = [image_to(first)] if relay else [image_to(d) for d in range(1, n_chip)]
    row_copies = []
    for d in range(1, n_tile):
        row_copies.append(to_tile(
            cov_rows.at[z], cov_rows.at[z], row_send.at[d - 1], row_recv.at[z],
            (z + d) % n_tile,
        ))
    for copy in start_now + [to_sibling] + cov_copies + row_copies:
        copy.start()

    def image_block(block):
        return to_epoch(
            held.at[block], held.at[block], pass_send.at[0], img_recv.at[block], sibling
        )

    def hand_over(d):
        block = partner(d) * 2 + core
        return to_epoch(
            held.at[block], held.at[block], pass_send.at[d], img_recv.at[block], sibling
        )

    half = rows // 2

    def relay_copy(d):
        block = partner(d) * 2 + core
        part = held.at[block, pl.ds(pl.multiple_of((d - 1) * half, half), half)]
        return to_epoch(
            part, part, relay_send.at[d - 1], relay_recv.at[d - 1],
            partner(3 - d) * 2 + core,
        )

    def relay_arrived(d):
        block = partner(3) * 2 + core
        part = held.at[block, pl.ds((d - 1) * half, half)]
        return to_epoch(
            part, part, relay_send.at[d - 1], relay_recv.at[d - 1],
            partner(3 - d) * 2 + core,
        )

    def pass_on(d):
        image_block(partner(d) * 2 + core).wait_recv()
        hand_over(d).start()
        if relay:
            relay_copy(d).start()

    def up_copy(block, i, target):
        ref = up.at[block, i]
        return to_tile(ref, ref, up_send.at[block, i], up_recv.at[block, i], target)

    def down_copy(block, i, target):
        ref = down.at[block, i]
        return to_tile(ref, ref, down_send.at[block, i], down_recv.at[block, i], target)

    above, below = jnp.minimum(z + 1, n_tile - 1), jnp.maximum(z - 1, 0)

    fetch.wait()
    lane = lax.broadcasted_iota(jnp.int32, (rows, SEG), 1).astype(jnp.float32)
    down_lane = lax.broadcasted_iota(jnp.int32, (SEG, rows), 0).astype(jnp.float32)
    for s in range(segs):
        span = slice(s * SEG, (s + 1) * SEG)
        flag = down_lane < cov_turn[s:s + 1, :]
        image = held[me, :, span].astype(jnp.float32).T
        left[span, :rows] = jnp.where(flag, image, 0.0).astype(jnp.bfloat16)
        left[span, rows:] = jnp.where(flag, 1.0, 0.0).astype(jnp.bfloat16)

    outer = (chip % 2 + chip // 2) % 2 == 0 if relay else None

    def place(n):
        if not relay:
            return n // 2, (core + n) % 2
        near, late = n % 2, n // 4
        diagonal = jnp.where(outer, n // 2 == 2, n // 2 == 3)
        d = jnp.where(
            late == 0,
            jnp.where(n < 2, 0, jnp.where(near == 0, first, second)),
            jnp.where(diagonal, 3, 2 - near),
        )
        k = jnp.where((late == 0) | diagonal, (core + n) % 2, near)
        return d, k

    def compute(n):
        d, k = place(n)
        block = partner(d) * 2 + k

        @pl.when(n == 2)
        def _():
            if relay:
                pass_on(first)
                image_to(first).wait_send()
                image_to(second).start()
            else:
                for e in range(1, n_chip):
                    pass_on(e)

        if relay:
            @pl.when(n == 4)
            def _():
                pass_on(second)

            @pl.when((d == 3) & (k == core))
            def _():
                relay_arrived(1).wait_recv()
                relay_arrived(2).wait_recv()
                hand_over(3).start()

        @pl.when(k != core)
        def _():
            image_block(block).wait_recv()

        @pl.when(n == 1)
        def _():
            for e in range(1, n_epoch):
                other = (me + e) % n_epoch
                to_epoch(
                    cov_held.at[other], cov_held.at[other], cov_send.at[0],
                    cov_recv.at[other], other,
                ).wait_recv()
            for e in range(1, n_tile):
                target = (z + e) % n_tile
                for j in range(blocks):
                    to_tile(
                        cov_held.at[target * blocks + j], cov_cols.at[z, j],
                        col_send.at[e - 1, j], col_recv.at[z, j], target,
                    ).start()
            for j in range(blocks):
                cov_cols[z, j] = cov_held[z * blocks + j]

        cov_turn[:segs] = cov_held[block]
        cov_pad[...] = cov_turn[...].T
        for s in range(segs):
            cols = slice(s * SEG, (s + 1) * SEG)
            flag = lane < cov_pad[:, s:s + 1]
            masked = jnp.where(flag, held[block, :, cols].astype(jnp.float32), 0.0)
            right[:rows, cols] = masked.astype(jnp.bfloat16)
            right[rows:2 * rows, cols] = jnp.where(flag, 1.0, 0.0).astype(jnp.bfloat16)
            right[2 * rows:, cols] = (masked * masked).astype(jnp.bfloat16)

        sums = jnp.dot(right[...], left[...], preferred_element_type=jnp.float32)
        parts[block, 0] = sums[:rows, :rows]
        parts[block, 1] = sums[rows:2 * rows, :rows]
        parts[block, 2] = sums[:rows, rows:]
        parts[block, 3] = sums[2 * rows:, rows:]

        target = block // blocks

        @pl.when(z == target)
        def _():
            own[block % blocks] = parts[block]

        @pl.when((z == 0) & (target > 0))
        def _():
            up[block] = parts[block]
            for i in range(4):
                up_copy(block, i, above).start()

        @pl.when((z == n_tile - 1) & (target < n_tile - 1))
        def _():
            down[block] = parts[block]
            for i in range(4):
                down_copy(block, i, below).start()

    def forward(n):
        d, k = place(n)
        block = partner(d) * 2 + k
        target = block // blocks

        @pl.when((z > 0) & (z < target))
        def _():
            for i in range(4):
                up_copy(block, i, above).wait_recv()
                up[block, i] = up[block, i] + parts[block, i]
                up_copy(block, i, above).start()

        @pl.when((z < n_tile - 1) & (z > target))
        def _():
            for i in range(4):
                down_copy(block, i, below).wait_recv()
                down[block, i] = down[block, i] + parts[block, i]
                down_copy(block, i, below).start()

    def intersect():
        for e in range(1, n_tile):
            other = (z + e) % n_tile
            to_tile(
                cov_rows.at[other], cov_rows.at[other], row_send.at[0], row_recv.at[other], other
            ).wait_recv()
            for j in range(blocks):
                to_tile(
                    cov_cols.at[other, j], cov_cols.at[other, j], col_send.at[0, j],
                    col_recv.at[other, j], other,
                ).wait_recv()
        inter[...] = jnp.zeros_like(inter)

        def overlap(t, carry):
            for j in range(blocks):
                cov_turn[:segs] = cov_cols[t, j]
                cov_pad[...] = cov_turn[...].T
                total = inter[j]
                for s in range(segs):
                    total = total + jnp.minimum(cov_pad[:, s:s + 1], cov_rows[t, s:s + 1, :])
                inter[j] = total
            return carry

        lax.fori_loop(0, n_tile, overlap, 0)

    lag = 2

    def step(n, carry):
        @pl.when(n < n_epoch)
        def _():
            compute(n)

        @pl.when(n == n_epoch - 3)
        def _():
            intersect()

        @pl.when(n >= lag)
        def _():
            forward(n - lag)

        return carry

    lax.fori_loop(0, n_epoch + lag, step, 0)

    for j in range(blocks):
        block = z * blocks + j

        @pl.when(z > 0)
        def _():
            for i in range(4):
                up_copy(block, i, below).wait_recv()
            own[j] = own[j] + up[block]

        @pl.when(z < n_tile - 1)
        def _():
            for i in range(4):
                down_copy(block, i, above).wait_recv()
            own[j] = own[j] + down[block]

        cols = slice(j * rows, (j + 1) * rows)
        intersection = inter[j]
        cross, flux_i, flux_j, power_j = own[j, 0], own[j, 1], own[j, 2], own[j, 3]
        spread = intersection * power_j - flux_j * flux_j
        covariance = intersection * cross - flux_i * flux_j
        scale_ratio = covariance / (spread + intersection + 1.0)
        scale_out[:, cols] = scale_ratio.T
        sky_out[:, cols] = ((flux_i - scale_ratio * flux_j) / (intersection + 1.0)).T

    late = [image_to(second)] if relay else start_now
    for copy in late + [to_sibling] + cov_copies + row_copies:
        copy.wait_send()
    for d in range(1, n_chip):
        hand_over(d).wait_send()
    if relay:
        relay_copy(1).wait_send()
        relay_copy(2).wait_send()
    for e in range(1, n_tile):
        target = (z + e) % n_tile
        for j in range(blocks):
            to_tile(
                cov_held.at[target * blocks + j], cov_cols.at[z, j],
                col_send.at[e - 1, j], col_recv.at[z, j], target,
            ).wait_send()

    def drain(block, carry):
        target = block // blocks

        @pl.when(z < target)
        def _():
            for i in range(4):
                up_copy(block, i, above).wait_send()

        @pl.when(z > target)
        def _():
            for i in range(4):
                down_copy(block, i, below).wait_send()

        return carry

    lax.fori_loop(0, n_epoch, drain, 0)


def solution(mesh):
    n_epoch, n_tile = mesh.shape["epoch"], mesh.shape["tile"]

    def body(images, coverage):
        rows, pixels = images.shape
        segs = coverage.shape[1]
        width = rows * n_epoch // n_tile
        blocks = width // rows
        dma, f32 = pltpu.SemaphoreType.DMA, jnp.float32
        out = jax.ShapeDtypeStruct((rows, width), f32)
        vmem = pl.BlockSpec(memory_space=pltpu.VMEM)
        return pl.pallas_call(
            functools.partial(kernel, n_epoch, n_tile),
            out_shape=(out, out),
            in_specs=[pl.BlockSpec(memory_space=pl.ANY)] * 2,
            out_specs=(vmem, vmem),
            scratch_shapes=[
                pltpu.VMEM((n_epoch, rows, pixels), jnp.bfloat16),
                pltpu.VMEM((pixels, 2 * rows), jnp.bfloat16),
                pltpu.VMEM((3 * rows, pixels), jnp.bfloat16),
                pltpu.VMEM((n_epoch, 4, rows, rows), f32),
                pltpu.VMEM((blocks, 4, rows, rows), f32),
                pltpu.VMEM((n_epoch, 4, rows, rows), f32),
                pltpu.VMEM((n_epoch, 4, rows, rows), f32),
                pltpu.VMEM((segs, rows), jnp.int32),
                pltpu.VMEM((rows, SEG), f32),
                pltpu.VMEM((SEG, rows), f32),
                pltpu.VMEM((n_epoch, segs, rows), f32),
                pltpu.VMEM((n_tile, segs, rows), f32),
                pltpu.VMEM((n_tile, blocks, segs, rows), f32),
                pltpu.VMEM((blocks, rows, rows), f32),
                dma((2,)), dma((n_epoch // 2,)), dma((n_epoch,)), dma((n_epoch // 2,)),
                dma((2,)), dma((2,)), dma((n_epoch,)), dma((n_epoch,)),
                dma((n_tile,)), dma((n_tile,)),
                dma((n_tile, blocks)), dma((n_tile, blocks)),
                dma((n_epoch, 4)), dma((n_epoch, 4)), dma((n_epoch, 4)), dma((n_epoch, 4)),
            ],
            compiler_params=pltpu.CompilerParams(
                collective_id=0, has_side_effects=True, vmem_limit_bytes=62 * 1024 * 1024
            ),
        )(images, coverage.T)

    specs = (P("epoch", "tile"), P("epoch", "tile"))
    return jax.shard_map(body, mesh=mesh, in_specs=specs, out_specs=specs, check_vma=False)
```

```python
import functools

import jax
import jax.numpy as jnp
from jax import lax
from jax.experimental import pallas as pl
from jax.experimental.pallas import tpu as pltpu
from jax.sharding import PartitionSpec as P

SEG = 128
MESH = pl.DeviceIdType.MESH


def kernel(
    n_epoch, n_tile, images, coverage, scale_out, sky_out,
    held, left, right, parts, own, up, down,
    cov_own, cov_pad, cov_turn, cov_held, cov_rows, cov_cols, inter,
    local_sem, img_send, img_recv, pass_send, relay_send, relay_recv, cov_send, cov_recv,
    row_send, row_recv, col_send, col_recv, up_send, up_recv, down_send, down_recv,
):
    rows, pixels = images.shape
    segs = pixels // SEG
    n_chip = n_epoch // 2
    blocks = own.shape[0]
    relay = n_chip == 4
    me = lax.axis_index("epoch")
    z = lax.axis_index("tile")
    chip, core = me // 2, me % 2
    sibling = chip * 2 + (1 - core)

    def partner(d):
        other, bit = 0, 1
        while bit < n_chip:
            other = other + ((chip // bit + d // bit) % 2) * bit
            bit *= 2
        return other

    def to_epoch(src, dst, send, recv, target):
        return pltpu.make_async_remote_copy(
            src_ref=src, dst_ref=dst, send_sem=send, recv_sem=recv,
            device_id={"epoch": target}, device_id_type=MESH,
        )

    def to_tile(src, dst, send, recv, target):
        return pltpu.make_async_remote_copy(
            src_ref=src, dst_ref=dst, send_sem=send, recv_sem=recv,
            device_id={"tile": target}, device_id_type=MESH,
        )

    fetch_cov = pltpu.make_async_copy(coverage, cov_own, local_sem.at[1])
    fetch_cov.start()
    fetch = pltpu.make_async_copy(images, held.at[me], local_sem.at[0])
    fetch.start()
    barrier = pltpu.get_barrier_semaphore()
    for d in range(1, n_epoch):
        pl.semaphore_signal(
            barrier, inc=1, device_id={"epoch": (me + d) % n_epoch}, device_id_type=MESH
        )
    for d in range(1, n_tile):
        pl.semaphore_signal(
            barrier, inc=1, device_id={"tile": (z + d) % n_tile}, device_id_type=MESH
        )
    cov_turn[...] = jnp.zeros_like(cov_turn)
    fetch_cov.wait()
    cov_held[me] = cov_own[...].astype(jnp.float32)
    cov_rows[z] = cov_held[me]
    cov_turn[:segs] = cov_held[me]
    cov_pad[...] = cov_turn[...].T
    pl.semaphore_wait(barrier, n_epoch + n_tile - 2)

    cov_copies = []
    for d in range(1, n_epoch):
        cov_copies.append(to_epoch(
            cov_held.at[me], cov_held.at[me], cov_send.at[d - 1], cov_recv.at[me],
            (me + d) % n_epoch,
        ))
    def image_to(d):
        return to_epoch(
            images, held.at[me], img_send.at[d], img_recv.at[me], partner(d) * 2 + core
        )

    to_sibling = to_epoch(images, held.at[me], img_send.at[0], img_recv.at[me], sibling)
    first, second = 1 + core, 2 - core
    start_now = [image_to(first)] if relay else [image_to(d) for d in range(1, n_chip)]
    row_copies = []
    for d in range(1, n_tile):
        row_copies.append(to_tile(
            cov_rows.at[z], cov_rows.at[z], row_send.at[d - 1], row_recv.at[z],
            (z + d) % n_tile,
        ))
    for copy in start_now + [to_sibling] + cov_copies + row_copies:
        copy.start()

    def image_block(block):
        return to_epoch(
            held.at[block], held.at[block], pass_send.at[0], img_recv.at[block], sibling
        )

    def hand_over(d):
        block = partner(d) * 2 + core
        return to_epoch(
            held.at[block], held.at[block], pass_send.at[d], img_recv.at[block], sibling
        )

    half = rows // 2

    def relay_copy(d):
        block = partner(d) * 2 + core
        part = held.at[block, pl.ds(pl.multiple_of((d - 1) * half, half), half)]
        return to_epoch(
            part, part, relay_send.at[d - 1], relay_recv.at[d - 1],
            partner(3 - d) * 2 + core,
        )

    def relay_arrived(d):
        block = partner(3) * 2 + core
        part = held.at[block, pl.ds((d - 1) * half, half)]
        return to_epoch(
            part, part, relay_send.at[d - 1], relay_recv.at[d - 1],
            partner(3 - d) * 2 + core,
        )

    def pass_on(d):
        image_block(partner(d) * 2 + core).wait_recv()
        hand_over(d).start()
        if relay:
            relay_copy(d).start()

    def up_copy(block, i, target):
        ref = up.at[block, i]
        return to_tile(ref, ref, up_send.at[block, i], up_recv.at[block, i], target)

    def down_copy(block, i, target):
        ref = down.at[block, i]
        return to_tile(ref, ref, down_send.at[block, i], down_recv.at[block, i], target)

    above, below = jnp.minimum(z + 1, n_tile - 1), jnp.maximum(z - 1, 0)

    fetch.wait()
    lane = lax.broadcasted_iota(jnp.int32, (rows, SEG), 1).astype(jnp.float32)
    down_lane = lax.broadcasted_iota(jnp.int32, (SEG, rows), 0).astype(jnp.float32)
    for s in range(segs):
        span = slice(s * SEG, (s + 1) * SEG)
        flag = down_lane < cov_turn[s:s + 1, :]
        image = held[me, :, span].astype(jnp.float32).T
        left[span, :rows] = jnp.where(flag, image, 0.0).astype(jnp.bfloat16)
        left[span, rows:] = jnp.where(flag, 1.0, 0.0).astype(jnp.bfloat16)

    outer = (chip % 2 + chip // 2) % 2 == 0 if relay else None

    end = (z == 0) | (z == n_tile - 1)

    def place(n, early):
        if not relay:
            return n // 2, (core + n) % 2
        near, late = n % 2, n // 4
        diagonal = n // 2 == jnp.where(early, 2, 3)
        d = jnp.where(
            late == 0,
            jnp.where(n < 2, 0, jnp.where(near == 0, first, second)),
            jnp.where(diagonal, 3, 2 - near),
        )
        k = jnp.where((late == 0) | diagonal, (core + n) % 2, near)
        return d, k

    def compute(n):
        d, k = place(n, outer & end if relay else None)
        block = partner(d) * 2 + k

        @pl.when(n == 2)
        def _():
            if relay:
                pass_on(first)
                image_to(first).wait_send()
                image_to(second).start()
            else:
                for e in range(1, n_chip):
                    pass_on(e)

        if relay:
            @pl.when(n == 4)
            def _():
                pass_on(second)

            @pl.when((d == 3) & (k == core))
            def _():
                relay_arrived(1).wait_recv()
                relay_arrived(2).wait_recv()
                hand_over(3).start()

        @pl.when(k != core)
        def _():
            image_block(block).wait_recv()

        @pl.when(n == 1)
        def _():
            for e in range(1, n_epoch):
                other = (me + e) % n_epoch
                to_epoch(
                    cov_held.at[other], cov_held.at[other], cov_send.at[0],
                    cov_recv.at[other], other,
                ).wait_recv()
            for e in range(1, n_tile):
                target = (z + e) % n_tile
                for j in range(blocks):
                    to_tile(
                        cov_held.at[target * blocks + j], cov_cols.at[z, j],
                        col_send.at[e - 1, j], col_recv.at[z, j], target,
                    ).start()
            for j in range(blocks):
                cov_cols[z, j] = cov_held[z * blocks + j]

        cov_turn[:segs] = cov_held[block]
        cov_pad[...] = cov_turn[...].T
        for s in range(segs):
            cols = slice(s * SEG, (s + 1) * SEG)
            flag = lane < cov_pad[:, s:s + 1]
            masked = jnp.where(flag, held[block, :, cols].astype(jnp.float32), 0.0)
            right[:rows, cols] = masked.astype(jnp.bfloat16)
            right[rows:2 * rows, cols] = jnp.where(flag, 1.0, 0.0).astype(jnp.bfloat16)
            right[2 * rows:, cols] = (masked * masked).astype(jnp.bfloat16)

        sums = jnp.dot(right[...], left[...], preferred_element_type=jnp.float32)
        parts[block, 0] = sums[:rows, :rows]
        parts[block, 1] = sums[rows:2 * rows, :rows]
        parts[block, 2] = sums[:rows, rows:]
        parts[block, 3] = sums[2 * rows:, rows:]

        target = block // blocks

        @pl.when(z == target)
        def _():
            own[block % blocks] = parts[block]

        @pl.when((z == 0) & (target > 0))
        def _():
            up[block] = parts[block]
            for i in range(4):
                up_copy(block, i, above).start()

        @pl.when((z == n_tile - 1) & (target < n_tile - 1))
        def _():
            down[block] = parts[block]
            for i in range(4):
                down_copy(block, i, below).start()

    def forward(n):
        d, k = place(n, outer)
        block = partner(d) * 2 + k
        target = block // blocks

        @pl.when((z > 0) & (z < target))
        def _():
            for i in range(4):
                up_copy(block, i, above).wait_recv()
                up[block, i] = up[block, i] + parts[block, i]
                up_copy(block, i, above).start()

        @pl.when((z < n_tile - 1) & (z > target))
        def _():
            for i in range(4):
                down_copy(block, i, below).wait_recv()
                down[block, i] = down[block, i] + parts[block, i]
                down_copy(block, i, below).start()

    def intersect():
        for e in range(1, n_tile):
            other = (z + e) % n_tile
            to_tile(
                cov_rows.at[other], cov_rows.at[other], row_send.at[0], row_recv.at[other], other
            ).wait_recv()
            for j in range(blocks):
                to_tile(
                    cov_cols.at[other, j], cov_cols.at[other, j], col_send.at[0, j],
                    col_recv.at[other, j], other,
                ).wait_recv()
        inter[...] = jnp.zeros_like(inter)

        def overlap(t, carry):
            for j in range(blocks):
                cov_turn[:segs] = cov_cols[t, j]
                cov_pad[...] = cov_turn[...].T
                total = inter[j]
                for s in range(segs):
                    total = total + jnp.minimum(cov_pad[:, s:s + 1], cov_rows[t, s:s + 1, :])
                inter[j] = total
            return carry

        lax.fori_loop(0, n_tile, overlap, 0)

    lag = 4

    def step(n, carry):
        @pl.when(n < n_epoch)
        def _():
            compute(n)

        @pl.when(n == n_epoch - 3)
        def _():
            intersect()

        @pl.when(n >= lag)
        def _():
            forward(n - lag)

        return carry

    lax.fori_loop(0, n_epoch + lag, step, 0)

    for j in range(blocks):
        block = z * blocks + j

        @pl.when(z > 0)
        def _():
            for i in range(4):
                up_copy(block, i, below).wait_recv()
            own[j] = own[j] + up[block]

        @pl.when(z < n_tile - 1)
        def _():
            for i in range(4):
                down_copy(block, i, above).wait_recv()
            own[j] = own[j] + down[block]

        cols = slice(j * rows, (j + 1) * rows)
        intersection = inter[j]
        cross, flux_i, flux_j, power_j = own[j, 0], own[j, 1], own[j, 2], own[j, 3]
        spread = intersection * power_j - flux_j * flux_j
        covariance = intersection * cross - flux_i * flux_j
        scale_ratio = covariance / (spread + intersection + 1.0)
        scale_out[:, cols] = scale_ratio.T
        sky_out[:, cols] = ((flux_i - scale_ratio * flux_j) / (intersection + 1.0)).T

    late = [image_to(second)] if relay else start_now
    for copy in late + [to_sibling] + cov_copies + row_copies:
        copy.wait_send()
    for d in range(1, n_chip):
        hand_over(d).wait_send()
    if relay:
        relay_copy(1).wait_send()
        relay_copy(2).wait_send()
    for e in range(1, n_tile):
        target = (z + e) % n_tile
        for j in range(blocks):
            to_tile(
                cov_held.at[target * blocks + j], cov_cols.at[z, j],
                col_send.at[e - 1, j], col_recv.at[z, j], target,
            ).wait_send()

    def drain(block, carry):
        target = block // blocks

        @pl.when(z < target)
        def _():
            for i in range(4):
                up_copy(block, i, above).wait_send()

        @pl.when(z > target)
        def _():
            for i in range(4):
                down_copy(block, i, below).wait_send()

        return carry

    lax.fori_loop(0, n_epoch, drain, 0)


def solution(mesh):
    n_epoch, n_tile = mesh.shape["epoch"], mesh.shape["tile"]

    def body(images, coverage):
        rows, pixels = images.shape
        segs = coverage.shape[1]
        width = rows * n_epoch // n_tile
        blocks = width // rows
        dma, f32 = pltpu.SemaphoreType.DMA, jnp.float32
        out = jax.ShapeDtypeStruct((rows, width), f32)
        vmem = pl.BlockSpec(memory_space=pltpu.VMEM)
        return pl.pallas_call(
            functools.partial(kernel, n_epoch, n_tile),
            out_shape=(out, out),
            in_specs=[pl.BlockSpec(memory_space=pl.ANY)] * 2,
            out_specs=(vmem, vmem),
            scratch_shapes=[
                pltpu.VMEM((n_epoch, rows, pixels), jnp.bfloat16),
                pltpu.VMEM((pixels, 2 * rows), jnp.bfloat16),
                pltpu.VMEM((3 * rows, pixels), jnp.bfloat16),
                pltpu.VMEM((n_epoch, 4, rows, rows), f32),
                pltpu.VMEM((blocks, 4, rows, rows), f32),
                pltpu.VMEM((n_epoch, 4, rows, rows), f32),
                pltpu.VMEM((n_epoch, 4, rows, rows), f32),
                pltpu.VMEM((segs, rows), jnp.int32),
                pltpu.VMEM((rows, SEG), f32),
                pltpu.VMEM((SEG, rows), f32),
                pltpu.VMEM((n_epoch, segs, rows), f32),
                pltpu.VMEM((n_tile, segs, rows), f32),
                pltpu.VMEM((n_tile, blocks, segs, rows), f32),
                pltpu.VMEM((blocks, rows, rows), f32),
                dma((2,)), dma((n_epoch // 2,)), dma((n_epoch,)), dma((n_epoch // 2,)),
                dma((2,)), dma((2,)), dma((n_epoch,)), dma((n_epoch,)),
                dma((n_tile,)), dma((n_tile,)),
                dma((n_tile, blocks)), dma((n_tile, blocks)),
                dma((n_epoch, 4)), dma((n_epoch, 4)), dma((n_epoch, 4)), dma((n_epoch, 4)),
            ],
            compiler_params=pltpu.CompilerParams(
                collective_id=0, has_side_effects=True, vmem_limit_bytes=62 * 1024 * 1024
            ),
        )(images, coverage.T)

    specs = (P("epoch", "tile"), P("epoch", "tile"))
    return jax.shard_map(body, mesh=mesh, in_specs=specs, out_specs=specs, check_vma=False)
```

```python
import functools

import jax
import jax.numpy as jnp
from jax import lax
from jax.experimental import pallas as pl
from jax.experimental.pallas import tpu as pltpu
from jax.sharding import PartitionSpec as P

SEG = 128
MESH = pl.DeviceIdType.MESH


def kernel(
    n_epoch, n_tile, images, coverage, scale_out, sky_out,
    held, left, right, parts, own, up, down,
    cov_own, cov_turn, meet_turn, spread_out, cov_held, cov_rows, cov_cols, inter,
    local_sem, img_send, img_recv, pass_send, relay_send, relay_recv, cov_send, cov_recv,
    row_send, row_recv, col_send, col_recv, up_send, up_recv, down_send, down_recv,
):
    rows, pixels = images.shape
    segs = pixels // SEG
    n_chip = n_epoch // 2
    blocks = own.shape[0]
    relay = n_chip == 4
    me = lax.axis_index("epoch")
    z = lax.axis_index("tile")
    chip, core = me // 2, me % 2
    sibling = chip * 2 + (1 - core)

    def partner(d):
        other, bit = 0, 1
        while bit < n_chip:
            other = other + ((chip // bit + d // bit) % 2) * bit
            bit *= 2
        return other

    def to_epoch(src, dst, send, recv, target):
        return pltpu.make_async_remote_copy(
            src_ref=src, dst_ref=dst, send_sem=send, recv_sem=recv,
            device_id={"epoch": target}, device_id_type=MESH,
        )

    def to_tile(src, dst, send, recv, target):
        return pltpu.make_async_remote_copy(
            src_ref=src, dst_ref=dst, send_sem=send, recv_sem=recv,
            device_id={"tile": target}, device_id_type=MESH,
        )

    fetch_cov = pltpu.make_async_copy(coverage, cov_own, local_sem.at[1])
    fetch_cov.start()
    fetch = pltpu.make_async_copy(images, held.at[me], local_sem.at[0])
    fetch.start()
    barrier = pltpu.get_barrier_semaphore()
    for d in range(1, n_epoch):
        pl.semaphore_signal(
            barrier, inc=1, device_id={"epoch": (me + d) % n_epoch}, device_id_type=MESH
        )
    for d in range(1, n_tile):
        pl.semaphore_signal(
            barrier, inc=1, device_id={"tile": (z + d) % n_tile}, device_id_type=MESH
        )
    cov_turn[...] = jnp.zeros_like(cov_turn)
    fetch_cov.wait()
    cov_held[me] = cov_own[...].astype(jnp.float32)
    cov_rows[z] = cov_held[me]
    pixel = lax.broadcasted_iota(jnp.int32, (SEG, pixels), 1)
    line = lax.broadcasted_iota(jnp.int32, (SEG, pixels), 0)
    spread_out[...] = jnp.where(
        line == segs, -(pixel % SEG), jnp.where(line == pixel // SEG, 1, 0)
    ).astype(jnp.float32).astype(jnp.bfloat16)
    cov_turn[segs:segs + 8] = jnp.where(
        lax.broadcasted_iota(jnp.int32, (8, rows), 0) == 0, 1.0, 0.0
    )
    meet_turn[...] = jnp.zeros_like(meet_turn)
    cov_turn[:segs] = cov_held[me]
    pl.semaphore_wait(barrier, n_epoch + n_tile - 2)

    cov_copies = []
    for d in range(1, n_epoch):
        cov_copies.append(to_epoch(
            cov_held.at[me], cov_held.at[me], cov_send.at[d - 1], cov_recv.at[me],
            (me + d) % n_epoch,
        ))
    def image_to(d):
        return to_epoch(
            images, held.at[me], img_send.at[d], img_recv.at[me], partner(d) * 2 + core
        )

    to_sibling = to_epoch(images, held.at[me], img_send.at[0], img_recv.at[me], sibling)
    first, second = 1 + core, 2 - core
    start_now = [image_to(first)] if relay else [image_to(d) for d in range(1, n_chip)]
    row_copies = []
    for d in range(1, n_tile):
        row_copies.append(to_tile(
            cov_rows.at[z], cov_rows.at[z], row_send.at[d - 1], row_recv.at[z],
            (z + d) % n_tile,
        ))
    for copy in start_now + [to_sibling] + cov_copies + row_copies:
        copy.start()

    def image_block(block):
        return to_epoch(
            held.at[block], held.at[block], pass_send.at[0], img_recv.at[block], sibling
        )

    def hand_over(d):
        block = partner(d) * 2 + core
        return to_epoch(
            held.at[block], held.at[block], pass_send.at[d], img_recv.at[block], sibling
        )

    half = rows // 2

    def relay_copy(d):
        block = partner(d) * 2 + core
        part = held.at[block, pl.ds(pl.multiple_of((d - 1) * half, half), half)]
        return to_epoch(
            part, part, relay_send.at[d - 1], relay_recv.at[d - 1],
            partner(3 - d) * 2 + core,
        )

    def relay_arrived(d):
        block = partner(3) * 2 + core
        part = held.at[block, pl.ds((d - 1) * half, half)]
        return to_epoch(
            part, part, relay_send.at[d - 1], relay_recv.at[d - 1],
            partner(3 - d) * 2 + core,
        )

    def pass_on(d):
        image_block(partner(d) * 2 + core).wait_recv()
        hand_over(d).start()
        if relay:
            relay_copy(d).start()

    def up_copy(block, i, target):
        ref = up.at[block, i]
        return to_tile(ref, ref, up_send.at[block, i], up_recv.at[block, i], target)

    def down_copy(block, i, target):
        ref = down.at[block, i]
        return to_tile(ref, ref, down_send.at[block, i], down_recv.at[block, i], target)

    above, below = jnp.minimum(z + 1, n_tile - 1), jnp.maximum(z - 1, 0)

    fetch.wait()
    down_lane = lax.broadcasted_iota(jnp.int32, (SEG, rows), 0).astype(jnp.float32)
    for s in range(segs):
        span = slice(s * SEG, (s + 1) * SEG)
        flag = down_lane < cov_turn[s:s + 1, :]
        image = held[me, :, span].astype(jnp.float32).T
        left[span, :rows] = jnp.where(flag, image, 0.0).astype(jnp.bfloat16)
        left[span, rows:] = jnp.where(flag, 1.0, 0.0).astype(jnp.bfloat16)

    outer = (chip % 2 + chip // 2) % 2 == 0 if relay else None

    def place(n):
        if not relay:
            return n // 2, (core + n) % 2
        near, late = n % 2, n // 4
        diagonal = jnp.where(outer, n // 2 == 2, n // 2 == 3)
        d = jnp.where(
            late == 0,
            jnp.where(n < 2, 0, jnp.where(near == 0, first, second)),
            jnp.where(diagonal, 3, 2 - near),
        )
        k = jnp.where((late == 0) | diagonal, (core + n) % 2, near)
        return d, k

    def compute(n):
        d, k = place(n)
        block = partner(d) * 2 + k

        @pl.when(n == 2)
        def _():
            if relay:
                pass_on(first)
                image_to(first).wait_send()
                image_to(second).start()
            else:
                for e in range(1, n_chip):
                    pass_on(e)

        if relay:
            @pl.when(n == 4)
            def _():
                pass_on(second)

            @pl.when((d == 3) & (k == core))
            def _():
                relay_arrived(1).wait_recv()
                relay_arrived(2).wait_recv()
                hand_over(3).start()

        @pl.when(k != core)
        def _():
            image_block(block).wait_recv()

        @pl.when(n == 1)
        def _():
            for e in range(1, n_epoch):
                other = (me + e) % n_epoch
                to_epoch(
                    cov_held.at[other], cov_held.at[other], cov_send.at[0],
                    cov_recv.at[other], other,
                ).wait_recv()
            for e in range(1, n_tile):
                target = (z + e) % n_tile
                for j in range(blocks):
                    to_tile(
                        cov_held.at[target * blocks + j], cov_cols.at[z, j],
                        col_send.at[e - 1, j], col_recv.at[z, j], target,
                    ).start()
            for j in range(blocks):
                cov_cols[z, j] = cov_held[z * blocks + j]

        cov_turn[:segs] = cov_held[block]
        left_over = jnp.dot(
            cov_turn[...].T.astype(jnp.bfloat16), spread_out[...],
            preferred_element_type=jnp.float32,
        )
        flags = jnp.clip(left_over, 0.0, 1.0).astype(jnp.bfloat16)
        masked = held[block] * flags
        right[:rows] = masked
        right[rows:2 * rows] = flags
        wide = masked.astype(jnp.float32)
        right[2 * rows:] = (wide * wide).astype(jnp.bfloat16)

        sums = jnp.dot(right[...], left[...], preferred_element_type=jnp.float32)
        parts[block, 0] = sums[:rows, :rows]
        parts[block, 1] = sums[rows:2 * rows, :rows]
        parts[block, 2] = sums[:rows, rows:]
        parts[block, 3] = sums[2 * rows:, rows:]

        target = block // blocks

        @pl.when(z == target)
        def _():
            own[block % blocks] = parts[block]

        @pl.when((z == 0) & (target > 0))
        def _():
            up[block] = parts[block]
            for i in range(4):
                up_copy(block, i, above).start()

        @pl.when((z == n_tile - 1) & (target < n_tile - 1))
        def _():
            down[block] = parts[block]
            for i in range(4):
                down_copy(block, i, below).start()

    def forward(n):
        d, k = place(n)
        block = partner(d) * 2 + k
        target = block // blocks

        @pl.when((z > 0) & (z < target))
        def _():
            for i in range(4):
                up_copy(block, i, above).wait_recv()
                up[block, i] = up[block, i] + parts[block, i]
                up_copy(block, i, above).start()

        @pl.when((z < n_tile - 1) & (z > target))
        def _():
            for i in range(4):
                down_copy(block, i, below).wait_recv()
                down[block, i] = down[block, i] + parts[block, i]
                down_copy(block, i, below).start()

    def intersect():
        for e in range(1, n_tile):
            other = (z + e) % n_tile
            to_tile(
                cov_rows.at[other], cov_rows.at[other], row_send.at[0], row_recv.at[other], other
            ).wait_recv()
            for j in range(blocks):
                to_tile(
                    cov_cols.at[other, j], cov_cols.at[other, j], col_send.at[0, j],
                    col_recv.at[other, j], other,
                ).wait_recv()
        inter[...] = jnp.zeros_like(inter)

        def overlap(t, carry):
            for j in range(blocks):
                meet_turn[:segs] = cov_cols[t, j]
                across = jnp.dot(
                    meet_turn[...].T.astype(jnp.bfloat16), spread_out[...],
                    preferred_element_type=jnp.float32,
                )
                total = inter[j]
                for s in range(segs):
                    total = total + jnp.minimum(
                        across[:, s * SEG:s * SEG + rows], cov_rows[t, s:s + 1, :]
                    )
                inter[j] = total
            return carry

        lax.fori_loop(0, n_tile, overlap, 0)

    lag = 2

    def step(n, carry):
        @pl.when(n < n_epoch)
        def _():
            compute(n)

        @pl.when(n == n_epoch - 3)
        def _():
            intersect()

        @pl.when(n >= lag)
        def _():
            forward(n - lag)

        return carry

    lax.fori_loop(0, n_epoch + lag, step, 0)

    for j in range(blocks):
        block = z * blocks + j

        @pl.when(z > 0)
        def _():
            for i in range(4):
                up_copy(block, i, below).wait_recv()
            own[j] = own[j] + up[block]

        @pl.when(z < n_tile - 1)
        def _():
            for i in range(4):
                down_copy(block, i, above).wait_recv()
            own[j] = own[j] + down[block]

        cols = slice(j * rows, (j + 1) * rows)
        intersection = inter[j]
        cross, flux_i, flux_j, power_j = own[j, 0], own[j, 1], own[j, 2], own[j, 3]
        spread = intersection * power_j - flux_j * flux_j
        covariance = intersection * cross - flux_i * flux_j
        scale_ratio = covariance / (spread + intersection + 1.0)
        scale_out[:, cols] = scale_ratio.T
        sky_out[:, cols] = ((flux_i - scale_ratio * flux_j) / (intersection + 1.0)).T

    late = [image_to(second)] if relay else start_now
    for copy in late + [to_sibling] + cov_copies + row_copies:
        copy.wait_send()
    for d in range(1, n_chip):
        hand_over(d).wait_send()
    if relay:
        relay_copy(1).wait_send()
        relay_copy(2).wait_send()
    for e in range(1, n_tile):
        target = (z + e) % n_tile
        for j in range(blocks):
            to_tile(
                cov_held.at[target * blocks + j], cov_cols.at[z, j],
                col_send.at[e - 1, j], col_recv.at[z, j], target,
            ).wait_send()

    def drain(block, carry):
        target = block // blocks

        @pl.when(z < target)
        def _():
            for i in range(4):
                up_copy(block, i, above).wait_send()

        @pl.when(z > target)
        def _():
            for i in range(4):
                down_copy(block, i, below).wait_send()

        return carry

    lax.fori_loop(0, n_epoch, drain, 0)


def solution(mesh):
    n_epoch, n_tile = mesh.shape["epoch"], mesh.shape["tile"]

    def body(images, coverage):
        rows, pixels = images.shape
        segs = coverage.shape[1]
        width = rows * n_epoch // n_tile
        blocks = width // rows
        dma, f32 = pltpu.SemaphoreType.DMA, jnp.float32
        out = jax.ShapeDtypeStruct((rows, width), f32)
        vmem = pl.BlockSpec(memory_space=pltpu.VMEM)
        return pl.pallas_call(
            functools.partial(kernel, n_epoch, n_tile),
            out_shape=(out, out),
            in_specs=[pl.BlockSpec(memory_space=pl.ANY)] * 2,
            out_specs=(vmem, vmem),
            scratch_shapes=[
                pltpu.VMEM((n_epoch, rows, pixels), jnp.bfloat16),
                pltpu.VMEM((pixels, 2 * rows), jnp.bfloat16),
                pltpu.VMEM((3 * rows, pixels), jnp.bfloat16),
                pltpu.VMEM((n_epoch, 4, rows, rows), f32),
                pltpu.VMEM((blocks, 4, rows, rows), f32),
                pltpu.VMEM((n_epoch, 4, rows, rows), f32),
                pltpu.VMEM((n_epoch, 4, rows, rows), f32),
                pltpu.VMEM((segs, rows), jnp.int32),
                pltpu.VMEM((SEG, rows), f32),
                pltpu.VMEM((SEG, rows), f32),
                pltpu.VMEM((SEG, pixels), jnp.bfloat16),
                pltpu.VMEM((n_epoch, segs, rows), f32),
                pltpu.VMEM((n_tile, segs, rows), f32),
                pltpu.VMEM((n_tile, blocks, segs, rows), f32),
                pltpu.VMEM((blocks, rows, rows), f32),
                dma((2,)), dma((n_epoch // 2,)), dma((n_epoch,)), dma((n_epoch // 2,)),
                dma((2,)), dma((2,)), dma((n_epoch,)), dma((n_epoch,)),
                dma((n_tile,)), dma((n_tile,)),
                dma((n_tile, blocks)), dma((n_tile, blocks)),
                dma((n_epoch, 4)), dma((n_epoch, 4)), dma((n_epoch, 4)), dma((n_epoch, 4)),
            ],
            compiler_params=pltpu.CompilerParams(
                collective_id=0, has_side_effects=True, vmem_limit_bytes=62 * 1024 * 1024
            ),
        )(images, coverage.T)

    specs = (P("epoch", "tile"), P("epoch", "tile"))
    return jax.shard_map(body, mesh=mesh, in_specs=specs, out_specs=specs, check_vma=False)
```

```python
import functools

import jax
import jax.numpy as jnp
from jax import lax
from jax.experimental import pallas as pl
from jax.experimental.pallas import tpu as pltpu
from jax.sharding import PartitionSpec as P

SEG = 128
MESH = pl.DeviceIdType.MESH


def kernel(
    n_epoch, n_tile, images, coverage, scale_out, sky_out,
    held, left, right, parts, own, up, down,
    cov_own, cov_turn, meet_turn, spread_out, cov_held, cov_rows, cov_cols, inter,
    local_sem, img_send, img_recv, pass_send, relay_send, relay_recv, cov_send, cov_recv,
    row_send, row_recv, col_send, col_recv, up_send, up_recv, down_send, down_recv,
):
    rows, pixels = images.shape
    segs = pixels // SEG
    n_chip = n_epoch // 2
    blocks = own.shape[0]
    relay = n_chip == 4
    me = lax.axis_index("epoch")
    z = lax.axis_index("tile")
    chip, core = me // 2, me % 2
    sibling = chip * 2 + (1 - core)

    def partner(d):
        other, bit = 0, 1
        while bit < n_chip:
            other = other + ((chip // bit + d // bit) % 2) * bit
            bit *= 2
        return other

    def to_epoch(src, dst, send, recv, target):
        return pltpu.make_async_remote_copy(
            src_ref=src, dst_ref=dst, send_sem=send, recv_sem=recv,
            device_id={"epoch": target}, device_id_type=MESH,
        )

    def to_tile(src, dst, send, recv, target):
        return pltpu.make_async_remote_copy(
            src_ref=src, dst_ref=dst, send_sem=send, recv_sem=recv,
            device_id={"tile": target}, device_id_type=MESH,
        )

    fetch_cov = pltpu.make_async_copy(coverage, cov_own, local_sem.at[1])
    fetch_cov.start()
    fetch = pltpu.make_async_copy(images, held.at[me], local_sem.at[0])
    fetch.start()
    barrier = pltpu.get_barrier_semaphore()
    for d in range(1, n_epoch):
        pl.semaphore_signal(
            barrier, inc=1, device_id={"epoch": (me + d) % n_epoch}, device_id_type=MESH
        )
    for d in range(1, n_tile):
        pl.semaphore_signal(
            barrier, inc=1, device_id={"tile": (z + d) % n_tile}, device_id_type=MESH
        )
    cov_turn[...] = jnp.zeros_like(cov_turn)
    fetch_cov.wait()
    cov_held[me] = cov_own[...].astype(jnp.float32)
    cov_rows[z] = cov_held[me]
    pixel = lax.broadcasted_iota(jnp.int32, (SEG, pixels), 1)
    line = lax.broadcasted_iota(jnp.int32, (SEG, pixels), 0)
    spread_out[...] = jnp.where(
        line == segs, -(pixel % SEG), jnp.where(line == pixel // SEG, 1, 0)
    ).astype(jnp.float32).astype(jnp.bfloat16)
    cov_turn[segs:segs + 8] = jnp.where(
        lax.broadcasted_iota(jnp.int32, (8, rows), 0) == 0, 1.0, 0.0
    )
    meet_turn[...] = jnp.zeros_like(meet_turn)
    cov_turn[:segs] = cov_held[me]
    pl.semaphore_wait(barrier, n_epoch + n_tile - 2)

    cov_copies = []
    for d in range(1, n_epoch):
        cov_copies.append(to_epoch(
            cov_held.at[me], cov_held.at[me], cov_send.at[d - 1], cov_recv.at[me],
            (me + d) % n_epoch,
        ))
    def image_to(d):
        return to_epoch(
            images, held.at[me], img_send.at[d], img_recv.at[me], partner(d) * 2 + core
        )

    to_sibling = to_epoch(images, held.at[me], img_send.at[0], img_recv.at[me], sibling)
    first, second = 1 + core, 2 - core
    start_now = [image_to(first)] if relay else [image_to(d) for d in range(1, n_chip)]
    row_copies = []
    for d in range(1, n_tile):
        row_copies.append(to_tile(
            cov_rows.at[z], cov_rows.at[z], row_send.at[d - 1], row_recv.at[z],
            (z + d) % n_tile,
        ))
    for copy in start_now + [to_sibling] + cov_copies + row_copies:
        copy.start()

    def image_block(block):
        return to_epoch(
            held.at[block], held.at[block], pass_send.at[0], img_recv.at[block], sibling
        )

    def hand_over(d):
        block = partner(d) * 2 + core
        return to_epoch(
            held.at[block], held.at[block], pass_send.at[d], img_recv.at[block], sibling
        )

    half = rows // 2

    def relay_copy(d):
        block = partner(d) * 2 + core
        part = held.at[block, pl.ds(pl.multiple_of((d - 1) * half, half), half)]
        return to_epoch(
            part, part, relay_send.at[d - 1], relay_recv.at[d - 1],
            partner(3 - d) * 2 + core,
        )

    def relay_arrived(d):
        block = partner(3) * 2 + core
        part = held.at[block, pl.ds((d - 1) * half, half)]
        return to_epoch(
            part, part, relay_send.at[d - 1], relay_recv.at[d - 1],
            partner(3 - d) * 2 + core,
        )

    def pass_on(d):
        image_block(partner(d) * 2 + core).wait_recv()
        hand_over(d).start()
        if relay:
            relay_copy(d).start()

    def up_copy(block, i, target):
        ref = up.at[block, i]
        return to_tile(ref, ref, up_send.at[block, i], up_recv.at[block, i], target)

    def down_copy(block, i, target):
        ref = down.at[block, i]
        return to_tile(ref, ref, down_send.at[block, i], down_recv.at[block, i], target)

    above, below = jnp.minimum(z + 1, n_tile - 1), jnp.maximum(z - 1, 0)

    fetch.wait()
    down_lane = lax.broadcasted_iota(jnp.int32, (SEG, rows), 0).astype(jnp.float32)
    for s in range(segs):
        span = slice(s * SEG, (s + 1) * SEG)
        flag = down_lane < cov_turn[s:s + 1, :]
        image = held[me, :, span].astype(jnp.float32).T
        left[span, :rows] = jnp.where(flag, image, 0.0).astype(jnp.bfloat16)
        left[span, rows:] = jnp.where(flag, 1.0, 0.0).astype(jnp.bfloat16)

    outer = (chip % 2 + chip // 2) % 2 == 0 if relay else None

    def place(n):
        if not relay:
            return n // 2, (core + n) % 2
        near, late = n % 2, n // 4
        diagonal = jnp.where(outer, n // 2 == 2, n // 2 == 3)
        d = jnp.where(
            late == 0,
            jnp.where(n < 2, 0, jnp.where(near == 0, first, second)),
            jnp.where(diagonal, 3, 2 - near),
        )
        k = jnp.where((late == 0) | diagonal, (core + n) % 2, near)
        return d, k

    def compute(n):
        d, k = place(n)
        block = partner(d) * 2 + k

        @pl.when(n == 2)
        def _():
            if relay:
                pass_on(first)
                image_to(first).wait_send()
                image_to(second).start()
            else:
                for e in range(1, n_chip):
                    pass_on(e)

        if relay:
            @pl.when(n == 4)
            def _():
                pass_on(second)

            @pl.when((d == 3) & (k == core))
            def _():
                relay_arrived(1).wait_recv()
                relay_arrived(2).wait_recv()
                hand_over(3).start()

        @pl.when(k != core)
        def _():
            image_block(block).wait_recv()

        @pl.when(n == 1)
        def _():
            for e in range(1, n_epoch):
                other = (me + e) % n_epoch
                to_epoch(
                    cov_held.at[other], cov_held.at[other], cov_send.at[0],
                    cov_recv.at[other], other,
                ).wait_recv()
            for e in range(1, n_tile):
                target = (z + e) % n_tile
                for j in range(blocks):
                    to_tile(
                        cov_held.at[target * blocks + j], cov_cols.at[z, j],
                        col_send.at[e - 1, j], col_recv.at[z, j], target,
                    ).start()
            for j in range(blocks):
                cov_cols[z, j] = cov_held[z * blocks + j]

        cov_turn[:segs] = cov_held[block]
        left_over = jnp.dot(
            cov_turn[...].T.astype(jnp.bfloat16), spread_out[...],
            preferred_element_type=jnp.float32,
        )
        flags = jnp.clip(left_over, 0.0, 1.0).astype(jnp.bfloat16)
        masked = held[block] * flags
        right[:rows] = masked
        right[rows:2 * rows] = flags
        wide = masked.astype(jnp.float32)
        right[2 * rows:] = (wide * wide).astype(jnp.bfloat16)

        sums = jnp.dot(right[...], left[...], preferred_element_type=jnp.float32)
        parts[block, 0] = sums[:rows, :rows]
        parts[block, 1] = sums[rows:2 * rows, :rows]
        parts[block, 2] = sums[:rows, rows:]
        parts[block, 3] = sums[2 * rows:, rows:]

        target = block // blocks

        @pl.when(z == target)
        def _():
            own[block % blocks] = parts[block]

        @pl.when((z == 0) & (target > 0))
        def _():
            up[block] = parts[block]
            for i in range(4):
                up_copy(block, i, above).start()

        @pl.when((z == n_tile - 1) & (target < n_tile - 1))
        def _():
            down[block] = parts[block]
            for i in range(4):
                down_copy(block, i, below).start()

    def forward(n):
        if relay:
            even = n - n % 2
            d, k = place(even)
            rising = jnp.where((partner(d) * 2 + k) // blocks > z, 1, 0)
            wanted = jnp.where(z < n_tile // 2, 1, 0)
            swap = (~outer) & (n >= 2) & (n < 6) & (rising != wanted)
            n = jnp.where(swap, even + 1 - n % 2, n)
        d, k = place(n)
        block = partner(d) * 2 + k
        target = block // blocks

        @pl.when((z > 0) & (z < target))
        def _():
            for i in range(4):
                up_copy(block, i, above).wait_recv()
                up[block, i] = up[block, i] + parts[block, i]
                up_copy(block, i, above).start()

        @pl.when((z < n_tile - 1) & (z > target))
        def _():
            for i in range(4):
                down_copy(block, i, below).wait_recv()
                down[block, i] = down[block, i] + parts[block, i]
                down_copy(block, i, below).start()

    def intersect():
        for e in range(1, n_tile):
            other = (z + e) % n_tile
            to_tile(
                cov_rows.at[other], cov_rows.at[other], row_send.at[0], row_recv.at[other], other
            ).wait_recv()
            for j in range(blocks):
                to_tile(
                    cov_cols.at[other, j], cov_cols.at[other, j], col_send.at[0, j],
                    col_recv.at[other, j], other,
                ).wait_recv()
        inter[...] = jnp.zeros_like(inter)

        def overlap(t, carry):
            for j in range(blocks):
                meet_turn[:segs] = cov_cols[t, j]
                across = jnp.dot(
                    meet_turn[...].T.astype(jnp.bfloat16), spread_out[...],
                    preferred_element_type=jnp.float32,
                )
                total = inter[j]
                for s in range(segs):
                    total = total + jnp.minimum(
                        across[:, s * SEG:s * SEG + rows], cov_rows[t, s:s + 1, :]
                    )
                inter[j] = total
            return carry

        lax.fori_loop(0, n_tile, overlap, 0)

    lag = 2

    def step(n, carry):
        @pl.when(n < n_epoch)
        def _():
            compute(n)

        @pl.when(n == n_epoch - 3)
        def _():
            intersect()

        @pl.when(n >= lag)
        def _():
            forward(n - lag)

        return carry

    lax.fori_loop(0, n_epoch + lag, step, 0)

    for j in range(blocks):
        block = z * blocks + j

        @pl.when(z > 0)
        def _():
            for i in range(4):
                up_copy(block, i, below).wait_recv()
            own[j] = own[j] + up[block]

        @pl.when(z < n_tile - 1)
        def _():
            for i in range(4):
                down_copy(block, i, above).wait_recv()
            own[j] = own[j] + down[block]

        cols = slice(j * rows, (j + 1) * rows)
        intersection = inter[j]
        cross, flux_i, flux_j, power_j = own[j, 0], own[j, 1], own[j, 2], own[j, 3]
        spread = intersection * power_j - flux_j * flux_j
        covariance = intersection * cross - flux_i * flux_j
        scale_ratio = covariance / (spread + intersection + 1.0)
        scale_out[:, cols] = scale_ratio.T
        sky_out[:, cols] = ((flux_i - scale_ratio * flux_j) / (intersection + 1.0)).T

    late = [image_to(second)] if relay else start_now
    for copy in late + [to_sibling] + cov_copies + row_copies:
        copy.wait_send()
    for d in range(1, n_chip):
        hand_over(d).wait_send()
    if relay:
        relay_copy(1).wait_send()
        relay_copy(2).wait_send()
    for e in range(1, n_tile):
        target = (z + e) % n_tile
        for j in range(blocks):
            to_tile(
                cov_held.at[target * blocks + j], cov_cols.at[z, j],
                col_send.at[e - 1, j], col_recv.at[z, j], target,
            ).wait_send()

    def drain(block, carry):
        target = block // blocks

        @pl.when(z < target)
        def _():
            for i in range(4):
                up_copy(block, i, above).wait_send()

        @pl.when(z > target)
        def _():
            for i in range(4):
                down_copy(block, i, below).wait_send()

        return carry

    lax.fori_loop(0, n_epoch, drain, 0)


def solution(mesh):
    n_epoch, n_tile = mesh.shape["epoch"], mesh.shape["tile"]

    def body(images, coverage):
        rows, pixels = images.shape
        segs = coverage.shape[1]
        width = rows * n_epoch // n_tile
        blocks = width // rows
        dma, f32 = pltpu.SemaphoreType.DMA, jnp.float32
        out = jax.ShapeDtypeStruct((rows, width), f32)
        vmem = pl.BlockSpec(memory_space=pltpu.VMEM)
        return pl.pallas_call(
            functools.partial(kernel, n_epoch, n_tile),
            out_shape=(out, out),
            in_specs=[pl.BlockSpec(memory_space=pl.ANY)] * 2,
            out_specs=(vmem, vmem),
            scratch_shapes=[
                pltpu.VMEM((n_epoch, rows, pixels), jnp.bfloat16),
                pltpu.VMEM((pixels, 2 * rows), jnp.bfloat16),
                pltpu.VMEM((3 * rows, pixels), jnp.bfloat16),
                pltpu.VMEM((n_epoch, 4, rows, rows), f32),
                pltpu.VMEM((blocks, 4, rows, rows), f32),
                pltpu.VMEM((n_epoch, 4, rows, rows), f32),
                pltpu.VMEM((n_epoch, 4, rows, rows), f32),
                pltpu.VMEM((segs, rows), jnp.int32),
                pltpu.VMEM((SEG, rows), f32),
                pltpu.VMEM((SEG, rows), f32),
                pltpu.VMEM((SEG, pixels), jnp.bfloat16),
                pltpu.VMEM((n_epoch, segs, rows), f32),
                pltpu.VMEM((n_tile, segs, rows), f32),
                pltpu.VMEM((n_tile, blocks, segs, rows), f32),
                pltpu.VMEM((blocks, rows, rows), f32),
                dma((2,)), dma((n_epoch // 2,)), dma((n_epoch,)), dma((n_epoch // 2,)),
                dma((2,)), dma((2,)), dma((n_epoch,)), dma((n_epoch,)),
                dma((n_tile,)), dma((n_tile,)),
                dma((n_tile, blocks)), dma((n_tile, blocks)),
                dma((n_epoch, 4)), dma((n_epoch, 4)), dma((n_epoch, 4)), dma((n_epoch, 4)),
            ],
            compiler_params=pltpu.CompilerParams(
                collective_id=0, has_side_effects=True, vmem_limit_bytes=62 * 1024 * 1024
            ),
        )(images, coverage.T)

    specs = (P("epoch", "tile"), P("epoch", "tile"))
    return jax.shard_map(body, mesh=mesh, in_specs=specs, out_specs=specs, check_vma=False)
```

```python
import functools

import jax
import jax.numpy as jnp
from jax import lax
from jax.experimental import pallas as pl
from jax.experimental.pallas import tpu as pltpu
from jax.sharding import PartitionSpec as P

SEG = 128
MESH = pl.DeviceIdType.MESH


def kernel(
    n_epoch, n_tile, images, coverage, scale_out, sky_out,
    held, left, right, parts, own, up, down,
    cov_own, cov_turn, meet_turn, spread_out, cov_held, cov_rows, cov_cols, inter,
    local_sem, img_send, img_recv, pass_send, relay_send, relay_recv, cov_send, cov_recv,
    row_send, row_recv, col_send, col_recv, up_send, up_recv, down_send, down_recv,
):
    rows, pixels = images.shape
    segs = pixels // SEG
    n_chip = n_epoch // 2
    blocks = own.shape[0]
    relay = n_chip == 4
    me = lax.axis_index("epoch")
    z = lax.axis_index("tile")
    chip, core = me // 2, me % 2
    sibling = chip * 2 + (1 - core)

    def partner(d):
        other, bit = 0, 1
        while bit < n_chip:
            other = other + ((chip // bit + d // bit) % 2) * bit
            bit *= 2
        return other

    def to_epoch(src, dst, send, recv, target):
        return pltpu.make_async_remote_copy(
            src_ref=src, dst_ref=dst, send_sem=send, recv_sem=recv,
            device_id={"epoch": target}, device_id_type=MESH,
        )

    def to_tile(src, dst, send, recv, target):
        return pltpu.make_async_remote_copy(
            src_ref=src, dst_ref=dst, send_sem=send, recv_sem=recv,
            device_id={"tile": target}, device_id_type=MESH,
        )

    fetch_cov = pltpu.make_async_copy(coverage, cov_own, local_sem.at[1])
    fetch_cov.start()
    fetch = pltpu.make_async_copy(images, held.at[me], local_sem.at[0])
    fetch.start()
    barrier = pltpu.get_barrier_semaphore()
    for d in range(1, n_epoch):
        pl.semaphore_signal(
            barrier, inc=1, device_id={"epoch": (me + d) % n_epoch}, device_id_type=MESH
        )
    for d in range(1, n_tile):
        pl.semaphore_signal(
            barrier, inc=1, device_id={"tile": (z + d) % n_tile}, device_id_type=MESH
        )
    pl.semaphore_wait(barrier, n_epoch + n_tile - 2)

    def image_to(d):
        return to_epoch(
            images, held.at[me], img_send.at[d], img_recv.at[me], partner(d) * 2 + core
        )

    to_sibling = to_epoch(images, held.at[me], img_send.at[0], img_recv.at[me], sibling)
    first, second = 1 + core, 2 - core
    start_now = [image_to(first)] if relay else [image_to(d) for d in range(1, n_chip)]
    for copy in start_now + [to_sibling]:
        copy.start()

    cov_turn[...] = jnp.zeros_like(cov_turn)
    fetch_cov.wait()
    cov_held[me] = cov_own[...].astype(jnp.float32)
    cov_rows[z] = cov_held[me]

    cov_copies = []
    for d in range(1, n_epoch):
        cov_copies.append(to_epoch(
            cov_held.at[me], cov_held.at[me], cov_send.at[d - 1], cov_recv.at[me],
            (me + d) % n_epoch,
        ))
    row_copies = []
    for d in range(1, n_tile):
        row_copies.append(to_tile(
            cov_rows.at[z], cov_rows.at[z], row_send.at[d - 1], row_recv.at[z],
            (z + d) % n_tile,
        ))
    for copy in cov_copies + row_copies:
        copy.start()

    pixel = lax.broadcasted_iota(jnp.int32, (SEG, pixels), 1)
    line = lax.broadcasted_iota(jnp.int32, (SEG, pixels), 0)
    spread_out[...] = jnp.where(
        line == segs, -(pixel % SEG), jnp.where(line == pixel // SEG, 1, 0)
    ).astype(jnp.float32).astype(jnp.bfloat16)
    cov_turn[segs:segs + 8] = jnp.where(
        lax.broadcasted_iota(jnp.int32, (8, rows), 0) == 0, 1.0, 0.0
    )
    meet_turn[...] = jnp.zeros_like(meet_turn)
    cov_turn[:segs] = cov_held[me]

    def image_block(block):
        return to_epoch(
            held.at[block], held.at[block], pass_send.at[0], img_recv.at[block], sibling
        )

    def hand_over(d):
        block = partner(d) * 2 + core
        return to_epoch(
            held.at[block], held.at[block], pass_send.at[d], img_recv.at[block], sibling
        )

    half = rows // 2

    def relay_copy(d):
        block = partner(d) * 2 + core
        part = held.at[block, pl.ds(pl.multiple_of((d - 1) * half, half), half)]
        return to_epoch(
            part, part, relay_send.at[d - 1], relay_recv.at[d - 1],
            partner(3 - d) * 2 + core,
        )

    def relay_arrived(d):
        block = partner(3) * 2 + core
        part = held.at[block, pl.ds((d - 1) * half, half)]
        return to_epoch(
            part, part, relay_send.at[d - 1], relay_recv.at[d - 1],
            partner(3 - d) * 2 + core,
        )

    def pass_on(d):
        image_block(partner(d) * 2 + core).wait_recv()
        hand_over(d).start()
        if relay:
            relay_copy(d).start()

    def up_copy(block, i, target):
        ref = up.at[block, i]
        return to_tile(ref, ref, up_send.at[block, i], up_recv.at[block, i], target)

    def down_copy(block, i, target):
        ref = down.at[block, i]
        return to_tile(ref, ref, down_send.at[block, i], down_recv.at[block, i], target)

    above, below = jnp.minimum(z + 1, n_tile - 1), jnp.maximum(z - 1, 0)

    fetch.wait()
    down_lane = lax.broadcasted_iota(jnp.int32, (SEG, rows), 0).astype(jnp.float32)
    for s in range(segs):
        span = slice(s * SEG, (s + 1) * SEG)
        flag = down_lane < cov_turn[s:s + 1, :]
        image = held[me, :, span].astype(jnp.float32).T
        left[span, :rows] = jnp.where(flag, image, 0.0).astype(jnp.bfloat16)
        left[span, rows:] = jnp.where(flag, 1.0, 0.0).astype(jnp.bfloat16)

    outer = (chip % 2 + chip // 2) % 2 == 0 if relay else None

    def place(n):
        if not relay:
            return n // 2, (core + n) % 2
        near, late = n % 2, n // 4
        diagonal = jnp.where(outer, n // 2 == 2, n // 2 == 3)
        d = jnp.where(
            late == 0,
            jnp.where(n < 2, 0, jnp.where(near == 0, first, second)),
            jnp.where(diagonal, 3, 2 - near),
        )
        k = jnp.where((late == 0) | diagonal, (core + n) % 2, near)
        return d, k

    def compute(n):
        d, k = place(n)
        block = partner(d) * 2 + k

        @pl.when(n == 2)
        def _():
            if relay:
                pass_on(first)
                image_to(first).wait_send()
                image_to(second).start()
            else:
                for e in range(1, n_chip):
                    pass_on(e)

        if relay:
            @pl.when(n == 4)
            def _():
                pass_on(second)

            @pl.when((d == 3) & (k == core))
            def _():
                relay_arrived(1).wait_recv()
                relay_arrived(2).wait_recv()
                hand_over(3).start()

        @pl.when(k != core)
        def _():
            image_block(block).wait_recv()

        @pl.when(n == 1)
        def _():
            for e in range(1, n_epoch):
                other = (me + e) % n_epoch
                to_epoch(
                    cov_held.at[other], cov_held.at[other], cov_send.at[0],
                    cov_recv.at[other], other,
                ).wait_recv()
            for e in range(1, n_tile):
                target = (z + e) % n_tile
                for j in range(blocks):
                    to_tile(
                        cov_held.at[target * blocks + j], cov_cols.at[z, j],
                        col_send.at[e - 1, j], col_recv.at[z, j], target,
                    ).start()
            for j in range(blocks):
                cov_cols[z, j] = cov_held[z * blocks + j]

        cov_turn[:segs] = cov_held[block]
        left_over = jnp.dot(
            cov_turn[...].T.astype(jnp.bfloat16), spread_out[...],
            preferred_element_type=jnp.float32,
        )
        flags = jnp.clip(left_over, 0.0, 1.0).astype(jnp.bfloat16)
        masked = held[block] * flags
        right[:rows] = masked
        right[rows:2 * rows] = flags
        wide = masked.astype(jnp.float32)
        right[2 * rows:] = (wide * wide).astype(jnp.bfloat16)

        sums = jnp.dot(right[...], left[...], preferred_element_type=jnp.float32)
        parts[block, 0] = sums[:rows, :rows]
        parts[block, 1] = sums[rows:2 * rows, :rows]
        parts[block, 2] = sums[:rows, rows:]
        parts[block, 3] = sums[2 * rows:, rows:]

        target = block // blocks

        @pl.when(z == target)
        def _():
            own[block % blocks] = parts[block]

        @pl.when((z == 0) & (target > 0))
        def _():
            up[block] = parts[block]
            for i in range(4):
                up_copy(block, i, above).start()

        @pl.when((z == n_tile - 1) & (target < n_tile - 1))
        def _():
            down[block] = parts[block]
            for i in range(4):
                down_copy(block, i, below).start()

    def forward(n):
        if relay:
            even = n - n % 2
            d, k = place(even)
            rising = jnp.where((partner(d) * 2 + k) // blocks > z, 1, 0)
            wanted = jnp.where(z < n_tile // 2, 1, 0)
            swap = (~outer) & (n >= 2) & (n < 6) & (rising != wanted)
            n = jnp.where(swap, even + 1 - n % 2, n)
        d, k = place(n)
        block = partner(d) * 2 + k
        target = block // blocks

        @pl.when((z > 0) & (z < target))
        def _():
            for i in range(4):
                up_copy(block, i, above).wait_recv()
                up[block, i] = up[block, i] + parts[block, i]
                up_copy(block, i, above).start()

        @pl.when((z < n_tile - 1) & (z > target))
        def _():
            for i in range(4):
                down_copy(block, i, below).wait_recv()
                down[block, i] = down[block, i] + parts[block, i]
                down_copy(block, i, below).start()

    def intersect():
        for e in range(1, n_tile):
            other = (z + e) % n_tile
            to_tile(
                cov_rows.at[other], cov_rows.at[other], row_send.at[0], row_recv.at[other], other
            ).wait_recv()
            for j in range(blocks):
                to_tile(
                    cov_cols.at[other, j], cov_cols.at[other, j], col_send.at[0, j],
                    col_recv.at[other, j], other,
                ).wait_recv()
        inter[...] = jnp.zeros_like(inter)

        def overlap(t, carry):
            for j in range(blocks):
                meet_turn[:segs] = cov_cols[t, j]
                across = jnp.dot(
                    meet_turn[...].T.astype(jnp.bfloat16), spread_out[...],
                    preferred_element_type=jnp.float32,
                )
                total = inter[j]
                for s in range(segs):
                    total = total + jnp.minimum(
                        across[:, s * SEG:s * SEG + rows], cov_rows[t, s:s + 1, :]
                    )
                inter[j] = total
            return carry

        lax.fori_loop(0, n_tile, overlap, 0)

    lag = 2

    def step(n, carry):
        @pl.when(n < n_epoch)
        def _():
            compute(n)

        @pl.when(n == n_epoch - 3)
        def _():
            intersect()

        @pl.when(n >= lag)
        def _():
            forward(n - lag)

        return carry

    lax.fori_loop(0, n_epoch + lag, step, 0)

    for j in range(blocks):
        block = z * blocks + j

        @pl.when(z > 0)
        def _():
            for i in range(4):
                up_copy(block, i, below).wait_recv()
            own[j] = own[j] + up[block]

        @pl.when(z < n_tile - 1)
        def _():
            for i in range(4):
                down_copy(block, i, above).wait_recv()
            own[j] = own[j] + down[block]

        cols = slice(j * rows, (j + 1) * rows)
        intersection = inter[j]
        cross, flux_i, flux_j, power_j = own[j, 0], own[j, 1], own[j, 2], own[j, 3]
        spread = intersection * power_j - flux_j * flux_j
        covariance = intersection * cross - flux_i * flux_j
        scale_ratio = covariance / (spread + intersection + 1.0)
        scale_out[:, cols] = scale_ratio.T
        sky_out[:, cols] = ((flux_i - scale_ratio * flux_j) / (intersection + 1.0)).T

    late = [image_to(second)] if relay else start_now
    for copy in late + [to_sibling] + cov_copies + row_copies:
        copy.wait_send()
    for d in range(1, n_chip):
        hand_over(d).wait_send()
    if relay:
        relay_copy(1).wait_send()
        relay_copy(2).wait_send()
    for e in range(1, n_tile):
        target = (z + e) % n_tile
        for j in range(blocks):
            to_tile(
                cov_held.at[target * blocks + j], cov_cols.at[z, j],
                col_send.at[e - 1, j], col_recv.at[z, j], target,
            ).wait_send()

    def drain(block, carry):
        target = block // blocks

        @pl.when(z < target)
        def _():
            for i in range(4):
                up_copy(block, i, above).wait_send()

        @pl.when(z > target)
        def _():
            for i in range(4):
                down_copy(block, i, below).wait_send()

        return carry

    lax.fori_loop(0, n_epoch, drain, 0)


def solution(mesh):
    n_epoch, n_tile = mesh.shape["epoch"], mesh.shape["tile"]

    def body(images, coverage):
        rows, pixels = images.shape
        segs = coverage.shape[1]
        width = rows * n_epoch // n_tile
        blocks = width // rows
        dma, f32 = pltpu.SemaphoreType.DMA, jnp.float32
        out = jax.ShapeDtypeStruct((rows, width), f32)
        vmem = pl.BlockSpec(memory_space=pltpu.VMEM)
        return pl.pallas_call(
            functools.partial(kernel, n_epoch, n_tile),
            out_shape=(out, out),
            in_specs=[pl.BlockSpec(memory_space=pl.ANY)] * 2,
            out_specs=(vmem, vmem),
            scratch_shapes=[
                pltpu.VMEM((n_epoch, rows, pixels), jnp.bfloat16),
                pltpu.VMEM((pixels, 2 * rows), jnp.bfloat16),
                pltpu.VMEM((3 * rows, pixels), jnp.bfloat16),
                pltpu.VMEM((n_epoch, 4, rows, rows), f32),
                pltpu.VMEM((blocks, 4, rows, rows), f32),
                pltpu.VMEM((n_epoch, 4, rows, rows), f32),
                pltpu.VMEM((n_epoch, 4, rows, rows), f32),
                pltpu.VMEM((segs, rows), jnp.int32),
                pltpu.VMEM((SEG, rows), f32),
                pltpu.VMEM((SEG, rows), f32),
                pltpu.VMEM((SEG, pixels), jnp.bfloat16),
                pltpu.VMEM((n_epoch, segs, rows), f32),
                pltpu.VMEM((n_tile, segs, rows), f32),
                pltpu.VMEM((n_tile, blocks, segs, rows), f32),
                pltpu.VMEM((blocks, rows, rows), f32),
                dma((2,)), dma((n_epoch // 2,)), dma((n_epoch,)), dma((n_epoch // 2,)),
                dma((2,)), dma((2,)), dma((n_epoch,)), dma((n_epoch,)),
                dma((n_tile,)), dma((n_tile,)),
                dma((n_tile, blocks)), dma((n_tile, blocks)),
                dma((n_epoch, 4)), dma((n_epoch, 4)), dma((n_epoch, 4)), dma((n_epoch, 4)),
            ],
            compiler_params=pltpu.CompilerParams(
                collective_id=0, has_side_effects=True, vmem_limit_bytes=62 * 1024 * 1024
            ),
        )(images, coverage.T)

    specs = (P("epoch", "tile"), P("epoch", "tile"))
    return jax.shard_map(body, mesh=mesh, in_specs=specs, out_specs=specs, check_vma=False)
```

```python
import functools

import jax
import jax.numpy as jnp
from jax import lax
from jax.experimental import pallas as pl
from jax.experimental.pallas import tpu as pltpu
from jax.sharding import PartitionSpec as P

SEG = 128
MESH = pl.DeviceIdType.MESH


def kernel(
    n_epoch, n_tile, images, coverage, scale_out, sky_out,
    held, left, right, parts, own, up, down,
    cov_own, cov_turn, meet_turn, spread_out, cov_held, cov_rows, cov_cols, inter,
    local_sem, img_send, img_recv, pass_send, relay_send, relay_recv, cov_send, cov_recv,
    row_send, row_recv, col_send, col_recv, up_send, up_recv, down_send, down_recv,
):
    rows, pixels = images.shape
    segs = pixels // SEG
    n_chip = n_epoch // 2
    blocks = own.shape[0]
    relay = n_chip == 4
    me = lax.axis_index("epoch")
    z = lax.axis_index("tile")
    chip, core = me // 2, me % 2
    sibling = chip * 2 + (1 - core)

    def partner(d):
        other, bit = 0, 1
        while bit < n_chip:
            other = other + ((chip // bit + d // bit) % 2) * bit
            bit *= 2
        return other

    def to_epoch(src, dst, send, recv, target):
        return pltpu.make_async_remote_copy(
            src_ref=src, dst_ref=dst, send_sem=send, recv_sem=recv,
            device_id={"epoch": target}, device_id_type=MESH,
        )

    def to_tile(src, dst, send, recv, target):
        return pltpu.make_async_remote_copy(
            src_ref=src, dst_ref=dst, send_sem=send, recv_sem=recv,
            device_id={"tile": target}, device_id_type=MESH,
        )

    fetch_cov = pltpu.make_async_copy(coverage, cov_own, local_sem.at[1])
    fetch_cov.start()
    fetch = pltpu.make_async_copy(images, held.at[me], local_sem.at[0])
    fetch.start()
    barrier = pltpu.get_barrier_semaphore()
    for d in range(1, n_epoch):
        pl.semaphore_signal(
            barrier, inc=1, device_id={"epoch": (me + d) % n_epoch}, device_id_type=MESH
        )
    for d in range(1, n_tile):
        pl.semaphore_signal(
            barrier, inc=1, device_id={"tile": (z + d) % n_tile}, device_id_type=MESH
        )
    cov_turn[...] = jnp.zeros_like(cov_turn)
    fetch_cov.wait()
    cov_held[me] = cov_own[...].astype(jnp.float32)
    cov_rows[z] = cov_held[me]
    pixel = lax.broadcasted_iota(jnp.int32, (SEG, pixels), 1)
    line = lax.broadcasted_iota(jnp.int32, (SEG, pixels), 0)
    spread_out[...] = jnp.where(
        line == segs, -(pixel % SEG), jnp.where(line == pixel // SEG, 1, 0)
    ).astype(jnp.float32).astype(jnp.bfloat16)
    cov_turn[segs:segs + 8] = jnp.where(
        lax.broadcasted_iota(jnp.int32, (8, rows), 0) == 0, 1.0, 0.0
    )
    meet_turn[...] = jnp.zeros_like(meet_turn)
    cov_turn[:segs] = cov_held[me]
    pl.semaphore_wait(barrier, n_epoch + n_tile - 2)

    cov_copies = []
    for d in range(1, n_epoch):
        cov_copies.append(to_epoch(
            cov_held.at[me], cov_held.at[me], cov_send.at[d - 1], cov_recv.at[me],
            (me + d) % n_epoch,
        ))
    def image_to(d):
        return to_epoch(
            images, held.at[me], img_send.at[d], img_recv.at[me], partner(d) * 2 + core
        )

    to_sibling = to_epoch(images, held.at[me], img_send.at[0], img_recv.at[me], sibling)
    first, second = 1 + core, 2 - core
    start_now = [image_to(first)] if relay else [image_to(d) for d in range(1, n_chip)]
    row_copies = []
    for d in range(1, n_tile):
        row_copies.append(to_tile(
            cov_rows.at[z], cov_rows.at[z], row_send.at[d - 1], row_recv.at[z],
            (z + d) % n_tile,
        ))
    for copy in start_now + [to_sibling] + cov_copies + row_copies:
        copy.start()

    def image_block(block):
        return to_epoch(
            held.at[block], held.at[block], pass_send.at[0], img_recv.at[block], sibling
        )

    def hand_over(d):
        block = partner(d) * 2 + core
        return to_epoch(
            held.at[block], held.at[block], pass_send.at[d], img_recv.at[block], sibling
        )

    half = rows // 2

    def relay_copy(d):
        block = partner(d) * 2 + core
        part = held.at[block, pl.ds(pl.multiple_of((d - 1) * half, half), half)]
        return to_epoch(
            part, part, relay_send.at[d - 1], relay_recv.at[d - 1],
            partner(3 - d) * 2 + core,
        )

    def relay_arrived(d):
        block = partner(3) * 2 + core
        part = held.at[block, pl.ds((d - 1) * half, half)]
        return to_epoch(
            part, part, relay_send.at[d - 1], relay_recv.at[d - 1],
            partner(3 - d) * 2 + core,
        )

    def pass_on(d):
        image_block(partner(d) * 2 + core).wait_recv()
        hand_over(d).start()
        if relay:
            relay_copy(d).start()

    def up_copy(block, i, target):
        ref = up.at[block, i]
        return to_tile(ref, ref, up_send.at[block, i], up_recv.at[block, i], target)

    def down_copy(block, i, target):
        ref = down.at[block, i]
        return to_tile(ref, ref, down_send.at[block, i], down_recv.at[block, i], target)

    above, below = jnp.minimum(z + 1, n_tile - 1), jnp.maximum(z - 1, 0)

    fetch.wait()
    down_lane = lax.broadcasted_iota(jnp.int32, (SEG, rows), 0).astype(jnp.float32)
    for s in range(segs):
        span = slice(s * SEG, (s + 1) * SEG)
        flag = down_lane < cov_turn[s:s + 1, :]
        image = held[me, :, span].astype(jnp.float32).T
        left[span, :rows] = jnp.where(flag, image, 0.0).astype(jnp.bfloat16)
        left[span, rows:] = jnp.where(flag, 1.0, 0.0).astype(jnp.bfloat16)

    outer = (chip % 2 + chip // 2) % 2 == 0 if relay else None

    def place(n):
        if not relay:
            return n // 2, (core + n) % 2
        near, late = n % 2, n // 4
        diagonal = jnp.where(outer, n // 2 == 2, n // 2 == 3)
        d = jnp.where(
            late == 0,
            jnp.where(n < 2, 0, jnp.where(near == 0, first, second)),
            jnp.where(diagonal, 3, 2 - near),
        )
        k = jnp.where((late == 0) | diagonal, (core + n) % 2, near)
        return d, k

    def compute(n):
        d, k = place(n)
        block = partner(d) * 2 + k

        @pl.when(n == 2)
        def _():
            if relay:
                pass_on(first)
                image_to(first).wait_send()
                image_to(second).start()
            else:
                for e in range(1, n_chip):
                    pass_on(e)

        if relay:
            @pl.when(n == 4)
            def _():
                pass_on(second)

            @pl.when((d == 3) & (k == core))
            def _():
                relay_arrived(1).wait_recv()
                relay_arrived(2).wait_recv()
                hand_over(3).start()

        @pl.when(k != core)
        def _():
            image_block(block).wait_recv()

        @pl.when(n == 1)
        def _():
            for e in range(1, n_epoch):
                other = (me + e) % n_epoch
                to_epoch(
                    cov_held.at[other], cov_held.at[other], cov_send.at[0],
                    cov_recv.at[other], other,
                ).wait_recv()
            for e in range(1, n_tile):
                target = (z + e) % n_tile
                for j in range(blocks):
                    to_tile(
                        cov_held.at[target * blocks + j], cov_cols.at[z, j],
                        col_send.at[e - 1, j], col_recv.at[z, j], target,
                    ).start()
            for j in range(blocks):
                cov_cols[z, j] = cov_held[z * blocks + j]

        cov_turn[:segs] = cov_held[block]
        left_over = jnp.dot(
            cov_turn[...].T.astype(jnp.bfloat16), spread_out[...],
            preferred_element_type=jnp.float32,
        )
        flags = jnp.clip(left_over, 0.0, 1.0).astype(jnp.bfloat16)
        masked = held[block] * flags
        right[:rows] = masked
        right[rows:2 * rows] = flags
        wide = masked.astype(jnp.float32)
        right[2 * rows:] = (wide * wide).astype(jnp.bfloat16)

        sums = jnp.dot(right[...], left[...], preferred_element_type=jnp.float32)
        parts[block, 0] = sums[:rows, :rows]
        parts[block, 1] = sums[rows:2 * rows, :rows]
        parts[block, 2] = sums[:rows, rows:]
        parts[block, 3] = sums[2 * rows:, rows:]

        target = block // blocks

        @pl.when(z == target)
        def _():
            own[block % blocks] = parts[block]

        @pl.when((z == 0) & (target > 0))
        def _():
            up[block] = parts[block]
            for i in range(4):
                up_copy(block, i, above).start()

        @pl.when((z == n_tile - 1) & (target < n_tile - 1))
        def _():
            down[block] = parts[block]
            for i in range(4):
                down_copy(block, i, below).start()

    def forward(n):
        if relay:
            even = n - n % 2
            d, k = place(even)
            rising = jnp.where((partner(d) * 2 + k) // blocks > z, 1, 0)
            wanted = jnp.where(z < n_tile // 2, 1, 0)
            swap = (~outer) & (n >= 2) & (n < 6) & (rising != wanted)
            n = jnp.where(swap, even + 1 - n % 2, n)
        d, k = place(n)
        block = partner(d) * 2 + k
        target = block // blocks

        @pl.when((z > 0) & (z < target))
        def _():
            for i in range(4):
                up_copy(block, i, above).wait_recv()
                up[block, i] = up[block, i] + parts[block, i]
                up_copy(block, i, above).start()

        @pl.when((z < n_tile - 1) & (z > target))
        def _():
            for i in range(4):
                down_copy(block, i, below).wait_recv()
                down[block, i] = down[block, i] + parts[block, i]
                down_copy(block, i, below).start()

    def intersect():
        for e in range(1, n_tile):
            other = (z + e) % n_tile
            to_tile(
                cov_rows.at[other], cov_rows.at[other], row_send.at[0], row_recv.at[other], other
            ).wait_recv()
            for j in range(blocks):
                to_tile(
                    cov_cols.at[other, j], cov_cols.at[other, j], col_send.at[0, j],
                    col_recv.at[other, j], other,
                ).wait_recv()
        inter[...] = jnp.zeros_like(inter)

        def overlap(t, carry):
            for j in range(blocks):
                meet_turn[:segs] = cov_cols[t, j]
                across = jnp.dot(
                    meet_turn[...].T.astype(jnp.bfloat16), spread_out[...],
                    preferred_element_type=jnp.float32,
                )
                total = inter[j]
                for s in range(segs):
                    total = total + jnp.minimum(
                        across[:, s * SEG:s * SEG + rows], cov_rows[t, s:s + 1, :]
                    )
                inter[j] = total
            return carry

        lax.fori_loop(0, n_tile, overlap, 0)

    lag = 1

    def step(n, carry):
        @pl.when(n < n_epoch)
        def _():
            compute(n)

        @pl.when(n == n_epoch - 3)
        def _():
            intersect()

        @pl.when(n >= lag)
        def _():
            forward(n - lag)

        return carry

    lax.fori_loop(0, n_epoch + lag, step, 0)

    for j in range(blocks):
        block = z * blocks + j

        @pl.when(z > 0)
        def _():
            for i in range(4):
                up_copy(block, i, below).wait_recv()
            own[j] = own[j] + up[block]

        @pl.when(z < n_tile - 1)
        def _():
            for i in range(4):
                down_copy(block, i, above).wait_recv()
            own[j] = own[j] + down[block]

        cols = slice(j * rows, (j + 1) * rows)
        intersection = inter[j]
        cross, flux_i, flux_j, power_j = own[j, 0], own[j, 1], own[j, 2], own[j, 3]
        spread = intersection * power_j - flux_j * flux_j
        covariance = intersection * cross - flux_i * flux_j
        scale_ratio = covariance / (spread + intersection + 1.0)
        scale_out[:, cols] = scale_ratio.T
        sky_out[:, cols] = ((flux_i - scale_ratio * flux_j) / (intersection + 1.0)).T

    late = [image_to(second)] if relay else start_now
    for copy in late + [to_sibling] + cov_copies + row_copies:
        copy.wait_send()
    for d in range(1, n_chip):
        hand_over(d).wait_send()
    if relay:
        relay_copy(1).wait_send()
        relay_copy(2).wait_send()
    for e in range(1, n_tile):
        target = (z + e) % n_tile
        for j in range(blocks):
            to_tile(
                cov_held.at[target * blocks + j], cov_cols.at[z, j],
                col_send.at[e - 1, j], col_recv.at[z, j], target,
            ).wait_send()

    def drain(block, carry):
        target = block // blocks

        @pl.when(z < target)
        def _():
            for i in range(4):
                up_copy(block, i, above).wait_send()

        @pl.when(z > target)
        def _():
            for i in range(4):
                down_copy(block, i, below).wait_send()

        return carry

    lax.fori_loop(0, n_epoch, drain, 0)


def solution(mesh):
    n_epoch, n_tile = mesh.shape["epoch"], mesh.shape["tile"]

    def body(images, coverage):
        rows, pixels = images.shape
        segs = coverage.shape[1]
        width = rows * n_epoch // n_tile
        blocks = width // rows
        dma, f32 = pltpu.SemaphoreType.DMA, jnp.float32
        out = jax.ShapeDtypeStruct((rows, width), f32)
        vmem = pl.BlockSpec(memory_space=pltpu.VMEM)
        return pl.pallas_call(
            functools.partial(kernel, n_epoch, n_tile),
            out_shape=(out, out),
            in_specs=[pl.BlockSpec(memory_space=pl.ANY)] * 2,
            out_specs=(vmem, vmem),
            scratch_shapes=[
                pltpu.VMEM((n_epoch, rows, pixels), jnp.bfloat16),
                pltpu.VMEM((pixels, 2 * rows), jnp.bfloat16),
                pltpu.VMEM((3 * rows, pixels), jnp.bfloat16),
                pltpu.VMEM((n_epoch, 4, rows, rows), f32),
                pltpu.VMEM((blocks, 4, rows, rows), f32),
                pltpu.VMEM((n_epoch, 4, rows, rows), f32),
                pltpu.VMEM((n_epoch, 4, rows, rows), f32),
                pltpu.VMEM((segs, rows), jnp.int32),
                pltpu.VMEM((SEG, rows), f32),
                pltpu.VMEM((SEG, rows), f32),
                pltpu.VMEM((SEG, pixels), jnp.bfloat16),
                pltpu.VMEM((n_epoch, segs, rows), f32),
                pltpu.VMEM((n_tile, segs, rows), f32),
                pltpu.VMEM((n_tile, blocks, segs, rows), f32),
                pltpu.VMEM((blocks, rows, rows), f32),
                dma((2,)), dma((n_epoch // 2,)), dma((n_epoch,)), dma((n_epoch // 2,)),
                dma((2,)), dma((2,)), dma((n_epoch,)), dma((n_epoch,)),
                dma((n_tile,)), dma((n_tile,)),
                dma((n_tile, blocks)), dma((n_tile, blocks)),
                dma((n_epoch, 4)), dma((n_epoch, 4)), dma((n_epoch, 4)), dma((n_epoch, 4)),
            ],
            compiler_params=pltpu.CompilerParams(
                collective_id=0, has_side_effects=True, vmem_limit_bytes=62 * 1024 * 1024
            ),
        )(images, coverage.T)

    specs = (P("epoch", "tile"), P("epoch", "tile"))
    return jax.shard_map(body, mesh=mesh, in_specs=specs, out_specs=specs, check_vma=False)
```
